128 devices in a mesh: outer: 4 (over z_lo, core), inner: 32 (over z_hi, x, y).
Axes of the slice: x: 4, y: 4, z: 4 (z_hi: 2, z_lo: 2; z = z_hi * 2 + z_lo), core: 2. Of those that a mesh axis runs over, the one named last changes fastest.
Arguments:
- queries: bfloat16 [16384, 512], P(('outer', 'inner')), may hold values from -2 to 2
- keys: bfloat16 [16384, 128], P(('outer', 'inner')), may hold values from -2 to 2
- values: bfloat16 [16384, 128], P(('outer', 'inner')), may hold values from -6 to 6
- saved_out: bfloat16 [16384, 512], P(('outer', 'inner')), may hold values from -4 to 4
- out_grad: bfloat16 [16384, 512], P(('outer', 'inner')), may hold values from -6 to 6
- log_sums: float32 [16384, 4], P(('outer', 'inner')), as said below
- positions: int32 [16384], P(('outer', 'inner')), may hold values from 0 to 16383, as said below
- segments: int32 [16384], P(('outer', 'inner')), may hold values from 0 to 8, as said below
Outputs:
- grad_queries: float32 [16384, 512], P(('outer', 'inner'))
- grad_keys: float32 [16384, 128], P(('outer', 'inner'))
- grad_values: float32 [16384, 128], P(('outer', 'inner'))
The draws below stay inside these ranges and needn't reach their ends.
Inputs may be any that keep to these rules, and one draw needn't show every extreme that they name: log_sums[i, h] is the log of the sum over allowed j of exp(scores_h[i, j]) for these queries, keys, positions and segments. A permutation of the positions; on every device the first 64 rows hold the consecutive positions of one block c of 64 positions, in order, and the last 64 rows those of block 255 - c. `segments`: document ids never fall as the position rises, position 0 has id 0, and each id from 0 to 8 occurs: nine documents.
All inputs are finite; a program needn't handle non-finite values.
Results may differ from the reference program's by a relative error of at most 0.0029.
Values may be sent and summed in bfloat16 or wider, within the bound.
No kernel may reach another device: no remote copies, remote signals or barrier semaphores. Data moves between devices by JAX's collectives and lax.ppermute only.
A program may use at most 192 MiB of HBM per device.

```python
import math
import jax
import jax.numpy as jnp
from jax import lax

HEAD = 128
QH = 4
TOK_DEV = 128
TOKENS = 16384


def layout(key):
    device_count = TOKENS // TOK_DEV
    half_rows = TOK_DEV // 2
    pair_index = jax.random.permutation(jax.random.fold_in(key, 101), device_count).astype(jnp.int32)
    row_index = jnp.arange(TOK_DEV, dtype=jnp.int32)[None, :]
    lower_run = pair_index[:, None]
    run_index = jnp.where(row_index < half_rows, lower_run, 2 * device_count - 1 - lower_run)
    stored_pos = (run_index * half_rows + row_index % half_rows).reshape(-1).astype(jnp.int32)
    order = jax.random.permutation(jax.random.fold_in(key, 102), TOKENS - 1).astype(jnp.int32)
    starts = order[:8] + 1
    all_pos = jnp.arange(TOKENS, dtype=jnp.int32)
    new_doc = jnp.any(all_pos[:, None] == starts[None, :], axis=1).astype(jnp.int32)
    doc_of_pos = jnp.cumsum(new_doc).astype(jnp.int32)
    return (stored_pos, doc_of_pos)


def query_key_rows(key, low_log):
    query_vals = jax.random.uniform(jax.random.fold_in(key, 201), (TOKENS, QH * HEAD), jnp.float32, -2.0, 2.0)
    key_vals = jax.random.uniform(jax.random.fold_in(key, 202), (TOKENS, HEAD), jnp.float32, -2.0, 2.0)
    query_scale = jnp.exp(jax.random.uniform(jax.random.fold_in(key, 203), (TOKENS, 1), jnp.float32, low_log, 0.0))
    key_scale = jnp.exp(jax.random.uniform(jax.random.fold_in(key, 204), (TOKENS, 1), jnp.float32, low_log, 0.0))
    return ((query_vals * query_scale).astype(jnp.bfloat16), (key_vals * key_scale).astype(jnp.bfloat16))


def draw_queries(key, part):
    low_log = 0.0
    query_rows, key_rows = query_key_rows(key, low_log)
    return query_rows


def draw_keys(key, part):
    low_log = 0.0
    query_rows, key_rows = query_key_rows(key, low_log)
    return key_rows


def draw_log_sums(key, part):
    low_log = 0.0
    query_rows, key_rows = query_key_rows(key, low_log)
    stored_pos, doc_of_pos = layout(key)
    stored_seg = doc_of_pos[stored_pos]
    query_all = query_rows.astype(jnp.float32)
    key_all = key_rows.astype(jnp.float32)
    block_len = math.gcd(TOKENS, 512)

    def one_block(block_idx):
        offset = block_idx * block_len
        query_block = lax.dynamic_slice_in_dim(query_all, offset, block_len, 0)
        pos_block = lax.dynamic_slice_in_dim(stored_pos, offset, block_len, 0)
        seg_block = lax.dynamic_slice_in_dim(stored_seg, offset, block_len, 0)
        allowed = (stored_pos[None, :] <= pos_block[:, None]) & (stored_seg[None, :] == seg_block[:, None])
        columns = []
        for head_idx in range(QH):
            query_head = query_block[:, head_idx * HEAD:(head_idx + 1) * HEAD]
            scores = jnp.dot(query_head, key_all.T, precision=lax.Precision.HIGHEST) * HEAD ** (-0.5)
            masked = jnp.where(allowed, scores, -1e+30)
            top = jnp.max(masked, axis=1)
            total = jnp.sum(jnp.where(allowed, jnp.exp(masked - top[:, None]), 0.0), axis=1)
            columns.append(top + jnp.log(total))
        return jnp.stack(columns, axis=1)
    blocks = lax.map(one_block, jnp.arange(TOKENS // block_len, dtype=jnp.int32))
    return blocks.reshape(TOKENS, QH).astype(jnp.float32)


def draw_positions(key, part):
    stored_pos, doc_of_pos = layout(key)
    return stored_pos


def draw_segments(key, part):
    stored_pos, doc_of_pos = layout(key)
    return doc_of_pos[stored_pos].astype(jnp.int32)


def level_of(key, extent, split, smallest, largest):
    level, own = 1.0, jax.random.fold_in(key, 6)
    for dim, shards_of in split:
        heights = jnp.exp(jax.random.uniform(jax.random.fold_in(own, dim), (shards_of,), jnp.float32, smallest / len(split), largest / len(split)))
        level = level * jnp.repeat(heights, extent[dim] // shards_of).reshape([-1 if axis == dim else 1 for axis in range(len(extent))])
    return level


def centred(key, shape, scale, reach, cuts=(), kind=jnp.bfloat16):
    loudness = level_of(key, shape, cuts, -0.22, 0.18) if cuts else 1.0
    array = jax.random.normal(key, shape, jnp.float32) * scale * loudness
    return jnp.minimum(jnp.maximum(array, -reach), reach).astype(kind)


def setup_inputs(seed: int = 0) -> dict:
    arg_keys = jax.random.split(jax.random.key(seed), 9)
    queries = draw_queries(jax.random.fold_in(arg_keys[8], 71), 0)
    keys = draw_keys(jax.random.fold_in(arg_keys[8], 71), 0)
    values = centred(arg_keys[2], (TOKENS, HEAD), 1.0, 6.0, ((0, 128),))
    saved_out = centred(arg_keys[3], (TOKENS, QH * HEAD), 0.3, 4.0, ((0, 128),))
    out_grad = centred(arg_keys[4], (TOKENS, QH * HEAD), 1.0, 6.0, ((0, 128),))
    log_sums = draw_log_sums(jax.random.fold_in(arg_keys[8], 71), 0)
    positions = draw_positions(jax.random.fold_in(arg_keys[8], 71), 0)
    segments = draw_segments(jax.random.fold_in(arg_keys[8], 71), 0)
    return {"queries": queries, "keys": keys, "values": values, "saved_out": saved_out, "out_grad": out_grad, "log_sums": log_sums, "positions": positions, "segments": segments}


def reference(queries, keys, values, saved_out, out_grad, log_sums, positions, segments):
    score_scale = HEAD ** -0.5
    block_len = math.gcd(TOKENS, 512)

    def one_block(state_pair, block_idx):
        grad_keys, grad_values = state_pair
        offset = block_idx * block_len
        query_block = lax.dynamic_slice_in_dim(queries, offset, block_len, 0)
        out_block = lax.dynamic_slice_in_dim(saved_out, offset, block_len, 0)
        grad_block = lax.dynamic_slice_in_dim(out_grad, offset, block_len, 0)
        lse_block = lax.dynamic_slice_in_dim(log_sums, offset, block_len, 0)
        pos_block = lax.dynamic_slice_in_dim(positions, offset, block_len, 0)
        seg_block = lax.dynamic_slice_in_dim(segments, offset, block_len, 0)
        allowed = (positions[None, :] <= pos_block[:, None]) & (segments[None, :] == seg_block[:, None])
        results = []
        for head_idx in range(QH):
            columns = slice(head_idx * HEAD, (head_idx + 1) * HEAD)
            query_head = query_block[:, columns]
            grad_head = grad_block[:, columns]
            scores = jnp.dot(query_head, keys.T, preferred_element_type=jnp.float32) * score_scale
            weights = jnp.where(allowed, jnp.exp(scores - lse_block[:, head_idx][:, None]), 0.0)
            rounded = weights.astype(jnp.bfloat16)
            out_dot = jnp.sum(grad_head.astype(jnp.float32) * out_block[:, columns].astype(jnp.float32), axis=1)
            grad_probs = jnp.dot(grad_head, values.T, preferred_element_type=jnp.float32)
            grad_scores = (weights * (grad_probs - out_dot[:, None]) * score_scale).astype(jnp.bfloat16)
            results.append(jnp.dot(grad_scores, keys, preferred_element_type=jnp.float32))
            grad_keys = grad_keys + jnp.dot(grad_scores.T, query_head, preferred_element_type=jnp.float32)
            grad_values = grad_values + jnp.dot(rounded.T, grad_head, preferred_element_type=jnp.float32)
        return (grad_keys, grad_values), jnp.concatenate(results, axis=1)

    empty = jnp.zeros((TOKENS, HEAD), jnp.float32)
    finals, grad_rows = lax.scan(one_block, (empty, empty), jnp.arange(TOKENS // block_len, dtype=jnp.int32))
    return grad_rows.reshape(TOKENS, QH * HEAD), finals[0], finals[1]
```

```python
import math

import jax
import jax.numpy as jnp
from jax import lax
from jax.experimental import pallas as pl
from jax.experimental.pallas import tpu as pltpu
from jax.sharding import PartitionSpec as P

HEAD = 128
QH = 4
ROWS = 128
BLOCK = 64
STATS = 16
PLANE = 16
DEPTH = 4
PIECES = 2 * DEPTH
QBLOCKS = 2 * PIECES
KBLOCKS = 2 * PLANE
STACK = QH * BLOCK
TILE = 256
FAR = 1.0e9
SPAN = 16384.0
AXES = ("outer", "inner")
LOG2E = math.log2(math.e)


def place(index):
    outer, inner = divmod(index, 32)
    return (inner // 16) * 2 + outer // 2, outer % 2, inner % 16


def index_of(z, core, spot):
    return ((z % 2) * 2 + core) * 32 + (z // 2) * 16 + spot


def along_z(array, shift):
    pairs = []
    for source in range(128):
        z, core, spot = place(source)
        pairs.append((source, index_of((z + shift) % DEPTH, core, spot)))
    return lax.ppermute(array, AXES, pairs)


def to_partner(array):
    pairs = []
    for source in range(128):
        z, core, spot = place(source)
        pairs.append((source, index_of(z, 1 - core, spot)))
    return lax.ppermute(array, AXES, pairs)


def over_plane(array):
    groups = [list(range(first, first + PLANE)) for first in (0, PLANE)]
    return lax.all_to_all(array, "inner", 0, 0, axis_index_groups=groups, tiled=True)


def pack_kernel(q_ref, g_ref, o_ref, k_ref, v_ref, lse_ref, pos_ref, seg_ref, qmsg_ref, kvmsg_ref):
    row = lax.broadcasted_iota(jnp.int32, (8, ROWS), 0)
    lane = lax.broadcasted_iota(jnp.int32, (8, ROWS), 1)
    block = jnp.right_shift(pos_ref[...], 6).astype(jnp.float32)
    seg = seg_ref[...].astype(jnp.float32)
    tops = []
    for h in range(QH):
        cols = slice(h * HEAD, (h + 1) * HEAD)
        prod = g_ref[:, cols].astype(jnp.float32) * o_ref[:, cols].astype(jnp.float32)
        dot = jnp.sum(prod.T, axis=0, keepdims=True)
        lse = jnp.broadcast_to(lse_ref[:, h : h + 1], (ROWS, ROWS)).T[0:1]
        tops.append(
            jnp.where(
                row == 0,
                lse,
                jnp.where(row == 1, dot, jnp.where(row == 2, block, jnp.where(row == 3, seg, 0.0))),
            )
        )
    qmsg_ref[0:ROWS, 0 : QH * HEAD] = q_ref[...]
    qmsg_ref[0:ROWS, QH * HEAD : 2 * QH * HEAD] = g_ref[...]
    for pair in range(2):
        first, second = tops[2 * pair], tops[2 * pair + 1]
        halves = (
            jnp.where(lane < BLOCK, first, pltpu.roll(second, BLOCK, 1)),
            jnp.where(lane < BLOCK, pltpu.roll(first, BLOCK, 1), second),
        )
        for b in range(2):
            full = halves[b]
            high = full.astype(jnp.bfloat16).astype(jnp.float32)
            middle = (full - high).astype(jnp.bfloat16).astype(jnp.float32)
            low = full - high - middle
            at = b * STACK + pair * ROWS
            qmsg_ref[ROWS : ROWS + STATS, at : at + ROWS] = jnp.concatenate(
                [high, middle], axis=0
            ).astype(jnp.bfloat16)
            qmsg_ref[ROWS : ROWS + STATS, at + 512 : at + 512 + ROWS] = jnp.concatenate(
                [low, jnp.zeros_like(low)], axis=0
            ).astype(jnp.bfloat16)
    tail = jnp.where(row == 0, block, jnp.where(row == 1, seg, 0.0))
    tail = jnp.concatenate([tail, jnp.zeros_like(tail)], axis=0).astype(jnp.bfloat16)
    for d in range(PLANE):
        kvmsg_ref[d, 0:ROWS, 0:HEAD] = k_ref[...]
        kvmsg_ref[d, 0:ROWS, HEAD : 2 * HEAD] = v_ref[...]
        kvmsg_ref[d, ROWS : ROWS + STATS, 0:ROWS] = tail
        kvmsg_ref[d, ROWS : ROWS + STATS, ROWS : 2 * ROWS] = jnp.zeros_like(tail)


def pack(queries, out_grad, saved_out, keys, values, log_sums, positions, segments):
    return pl.pallas_call(
        pack_kernel,
        out_shape=(
            jax.ShapeDtypeStruct((ROWS + STATS, 2 * QH * HEAD), jnp.bfloat16),
            jax.ShapeDtypeStruct((PLANE, ROWS + STATS, 2 * HEAD), jnp.bfloat16),
        ),
        in_specs=[pl.BlockSpec(memory_space=pltpu.VMEM)] * 8,
        out_specs=(pl.BlockSpec(memory_space=pltpu.VMEM),) * 2,
        compiler_params=pltpu.CompilerParams(vmem_limit_bytes=16 * 1024 * 1024),
        name="pack",
    )(
        queries,
        out_grad,
        saved_out,
        keys,
        values,
        log_sums,
        positions.reshape(1, ROWS),
        segments.reshape(1, ROWS),
    )


def grad_kernel(*refs):
    q_refs = refs[:PIECES]
    (kv_ref, dkv_ref, own_ref, other_ref) = refs[PIECES : PIECES + 4]
    (qs, gs, rows, kvs, kcode, dk, dv, dq, ints, ints_s, sem) = refs[PIECES + 4 :]
    scale = HEAD ** (-0.5)
    lane = lax.broadcasted_iota(jnp.int32, (1, ROWS), 1)
    inside = jnp.bitwise_and(lane, BLOCK - 1).astype(jnp.float32)

    codes = []
    for d in range(PLANE):
        tail = kv_ref[d, ROWS : ROWS + STATS, 0:ROWS].astype(jnp.float32)
        codes.append(tail[1:2] * SPAN + tail[0:1] * BLOCK + inside)
    code = jnp.concatenate(codes, axis=0)
    first = jnp.concatenate([code[:, 0:1], code[:, BLOCK : BLOCK + 1]], axis=0)
    last = jnp.concatenate([code[:, BLOCK - 1 : BLOCK], code[:, ROWS - 1 : ROWS]], axis=0)
    pad = jnp.full((ROWS - KBLOCKS, ROWS), FAR, jnp.float32)
    first_b = jnp.broadcast_to(first, (KBLOCKS, ROWS))
    first_t = jnp.concatenate([first_b, pad], axis=0).T
    last_t = jnp.concatenate([jnp.broadcast_to(last, (KBLOCKS, ROWS)), pad], axis=0).T
    rank = jnp.sum((first_t[0:KBLOCKS] < first_b).astype(jnp.float32), axis=1, keepdims=True)

    starts, ends = [], []
    for p in range(PIECES):
        tail = q_refs[p][ROWS : ROWS + STATS, :].astype(jnp.float32)
        stat = tail[0:8, 0:512] + tail[8:16, 0:512] + tail[0:8, 512:1024]
        for b in range(2):
            part = stat[:, b * STACK : (b + 1) * STACK]
            within = jnp.bitwise_and(
                lax.broadcasted_iota(jnp.int32, (1, STACK), 1), BLOCK - 1
            ).astype(jnp.float32)
            begin = part[3:4] * SPAN
            own = begin + part[2:3] * BLOCK + within
            rows[2 * p + b, 0:1, :] = part[0:1] * LOG2E
            rows[2 * p + b, 1:2, :] = part[1:2]
            rows[2 * p + b, 2:3, :] = begin
            rows[2 * p + b, 3:4, :] = own
            starts.append(begin[:, 0:1])
            ends.append(own[:, BLOCK - 1 : BLOCK])
    starts = jnp.concatenate(starts, axis=0)
    ends = jnp.concatenate(ends, axis=0)
    low = jnp.sum((last_t[0:QBLOCKS] < starts).astype(jnp.float32), axis=1, keepdims=True)
    high = jnp.sum((first_t[0:QBLOCKS] <= ends).astype(jnp.float32), axis=1, keepdims=True)
    empty = jnp.zeros((KBLOCKS - QBLOCKS, 1), jnp.float32)
    low = jnp.concatenate([low, empty], axis=0)
    high = jnp.concatenate([high, empty], axis=0)
    place_lane = lax.broadcasted_iota(jnp.int32, (KBLOCKS, ROWS), 1)
    ints[...] = jnp.where(place_lane == 0, rank, jnp.where(place_lane == 1, low, high)).astype(
        jnp.int32
    )
    copy = pltpu.make_async_copy(ints, ints_s, sem)
    copy.start()

    for p in range(PIECES):
        for b in range(2):
            for h in range(QH):
                to = slice(h * BLOCK, (h + 1) * BLOCK)
                frm = slice(b * BLOCK, (b + 1) * BLOCK)
                qs[2 * p + b, to, :] = q_refs[p][frm, h * HEAD : (h + 1) * HEAD]
                gs[2 * p + b, to, :] = q_refs[p][frm, (QH + h) * HEAD : (QH + h + 1) * HEAD]
    dk[...] = jnp.zeros_like(dk)
    dv[...] = jnp.zeros_like(dv)
    kvs[KBLOCKS * BLOCK :, :] = jnp.zeros((TILE, 2 * HEAD), jnp.bfloat16)
    kcode[KBLOCKS * BLOCK :, :] = jnp.full((TILE, ROWS), FAR, jnp.float32)

    copy.wait()
    for d in range(PLANE):
        column = jnp.broadcast_to(code[d : d + 1], (ROWS, ROWS)).T
        for b in range(2):
            at = pl.multiple_of(ints_s[b * PLANE + d, 0] * BLOCK, BLOCK)
            frm = slice(b * BLOCK, (b + 1) * BLOCK)
            kvs[pl.ds(at, BLOCK), :] = kv_ref[d, frm, :]
            kcode[pl.ds(at, BLOCK), :] = column[frm]

    def one_query_block(qi, carry):
        lower = ints_s[qi, 1]
        steps = jnp.right_shift(jnp.maximum(ints_s[qi, 2] - lower, 0) + 3, 2)
        dq[...] = jnp.zeros_like(dq)

        def one_tile(step, carry):
            at = pl.multiple_of((lower + step * (TILE // BLOCK)) * BLOCK, BLOCK)
            where = pl.ds(at, TILE)
            k = kvs[where, 0:HEAD]
            v = kvs[where, HEAD : 2 * HEAD]
            q = qs[qi]
            g = gs[qi]
            nt = (((1,), (1,)), ((), ()))
            s = lax.dot_general(k, q, nt, preferred_element_type=jnp.float32)
            gp = lax.dot_general(v, g, nt, preferred_element_type=jnp.float32)
            col = kcode[where, :]
            seen = (col >= rows[qi, 2:3, 0:ROWS]) & (col <= rows[qi, 3:4, 0:ROWS])
            seen = jnp.concatenate([seen, seen], axis=1)
            w = jnp.where(seen, jnp.exp2(s * (scale * LOG2E) - rows[qi, 0:1, :]), 0.0)
            ds = (w * (gp - rows[qi, 1:2, :]) * scale).astype(jnp.bfloat16)
            dv[where, :] += jnp.dot(w.astype(jnp.bfloat16), g, preferred_element_type=jnp.float32)
            dk[where, :] += jnp.dot(ds, q, preferred_element_type=jnp.float32)
            dq[...] += lax.dot_general(
                ds, k, (((0,), (0,)), ((), ())), preferred_element_type=jnp.float32
            )
            return carry

        lax.fori_loop(0, steps, one_tile, 0)
        piece = jnp.right_shift(qi, 1)
        to = pl.ds(pl.multiple_of(jnp.bitwise_and(qi, 1) * BLOCK, BLOCK), BLOCK)
        for h in range(QH):
            part = dq[h * BLOCK : (h + 1) * BLOCK, :]

            @pl.when(piece < DEPTH)
            def _():
                own_ref[piece, to, h * HEAD : (h + 1) * HEAD] = part

            @pl.when(piece >= DEPTH)
            def _():
                other_ref[piece - DEPTH, to, h * HEAD : (h + 1) * HEAD] = part.astype(jnp.bfloat16)

        return carry

    lax.fori_loop(0, QBLOCKS, one_query_block, 0)

    for d in range(PLANE):
        for b in range(2):
            at = pl.multiple_of(ints_s[b * PLANE + d, 0] * BLOCK, BLOCK)
            to = slice(b * BLOCK, (b + 1) * BLOCK)
            dkv_ref[d, to, 0:HEAD] = dk[pl.ds(at, BLOCK), :].astype(jnp.bfloat16)
            dkv_ref[d, to, HEAD : 2 * HEAD] = dv[pl.ds(at, BLOCK), :].astype(jnp.bfloat16)


def grads(pieces, kv):
    keys_room = KBLOCKS * BLOCK + TILE
    return pl.pallas_call(
        grad_kernel,
        out_shape=(
            jax.ShapeDtypeStruct((PLANE, ROWS, 2 * HEAD), jnp.bfloat16),
            jax.ShapeDtypeStruct((DEPTH, ROWS, QH * HEAD), jnp.float32),
            jax.ShapeDtypeStruct((DEPTH, ROWS, QH * HEAD), jnp.bfloat16),
        ),
        in_specs=[pl.BlockSpec(memory_space=pltpu.VMEM)] * (PIECES + 1),
        out_specs=(pl.BlockSpec(memory_space=pltpu.VMEM),) * 3,
        scratch_shapes=[
            pltpu.VMEM((QBLOCKS, STACK, HEAD), jnp.bfloat16),
            pltpu.VMEM((QBLOCKS, STACK, HEAD), jnp.bfloat16),
            pltpu.VMEM((QBLOCKS, 8, STACK), jnp.float32),
            pltpu.VMEM((keys_room, 2 * HEAD), jnp.bfloat16),
            pltpu.VMEM((keys_room, ROWS), jnp.float32),
            pltpu.VMEM((keys_room, HEAD), jnp.float32),
            pltpu.VMEM((keys_room, HEAD), jnp.float32),
            pltpu.VMEM((STACK, HEAD), jnp.float32),
            pltpu.VMEM((KBLOCKS, ROWS), jnp.int32),
            pltpu.SMEM((KBLOCKS, ROWS), jnp.int32),
            pltpu.SemaphoreType.DMA,
        ],
        compiler_params=pltpu.CompilerParams(vmem_limit_bytes=32 * 1024 * 1024),
        name="grads",
    )(*pieces, kv)


def body(queries, keys, values, saved_out, out_grad, log_sums, positions, segments):
    qmsg, kvmsg = pack(queries, out_grad, saved_out, keys, values, log_sums, positions, segments)
    column = [qmsg] + [along_z(qmsg, shift) for shift in (1, 2, 3)]
    kv = over_plane(kvmsg)
    column = column + [to_partner(piece) for piece in column]
    dkv, own, other = grads(column, kv)
    total = own + to_partner(other).astype(jnp.float32)
    back = [along_z(total[shift].astype(jnp.bfloat16), -shift) for shift in (1, 2, 3)]
    parts = over_plane(dkv)
    grad_kv = jnp.sum(parts.astype(jnp.float32), axis=0)
    grad_queries = total[0]
    for part in back:
        grad_queries = grad_queries + part.astype(jnp.float32)
    return (grad_queries, grad_kv[:, :HEAD], grad_kv[:, HEAD:])


def solution(mesh):
    rows2, rows1 = P(AXES, None), P(AXES)
    return jax.shard_map(
        body,
        mesh=mesh,
        in_specs=(rows2,) * 6 + (rows1,) * 2,
        out_specs=(rows2,) * 3,
        check_vma=False,
    )
```

```python
import math

import jax
import jax.numpy as jnp
from jax import lax
from jax.experimental import pallas as pl
from jax.experimental.pallas import tpu as pltpu
from jax.sharding import PartitionSpec as P

HEAD = 128
QH = 4
ROWS = 128
BLOCK = 64
STATS = 16
PLANE = 16
DEPTH = 4
PIECES = 2 * DEPTH
QBLOCKS = 2 * PIECES
KBLOCKS = 2 * PLANE
STACK = QH * BLOCK
TILE = 256
TILE_BLOCKS = TILE // BLOCK
SLOTS = 40
TOGETHER = 2
FAR = 1.0e9
AXES = ("outer", "inner")
LOG2E = math.log2(math.e)


def place(index):
    outer, inner = divmod(index, 32)
    return (inner // 16) * 2 + outer // 2, outer % 2, inner % 16


def index_of(z, core, spot):
    return ((z % 2) * 2 + core) * 32 + (z // 2) * 16 + spot


def along_z(array, shift):
    pairs = []
    for source in range(128):
        z, core, spot = place(source)
        pairs.append((source, index_of((z + shift) % DEPTH, core, spot)))
    return lax.ppermute(array, AXES, pairs)


def to_partner(array):
    pairs = []
    for source in range(128):
        z, core, spot = place(source)
        pairs.append((source, index_of(z, 1 - core, spot)))
    return lax.ppermute(array, AXES, pairs)


def over_plane(array):
    groups = [list(range(first, first + PLANE)) for first in (0, PLANE)]
    return lax.all_to_all(array, "inner", 0, 0, axis_index_groups=groups, tiled=True)


def pack_kernel(q_hbm, g_hbm, o_hbm, k_hbm, v_hbm, lse_hbm, pos_hbm, seg_hbm, qmsg_ref, kvmsg_ref, *scratch):
    (q_ref, g_ref, o_ref, k_ref, v_ref, lse_ref, pos_ref, seg_ref, sems) = scratch
    sources = (lse_hbm, pos_hbm, seg_hbm, g_hbm, o_hbm, q_hbm, k_hbm, v_hbm)
    targets = (lse_ref, pos_ref, seg_ref, g_ref, o_ref, q_ref, k_ref, v_ref)
    copies = [pltpu.make_async_copy(s, t, sems.at[i]) for i, (s, t) in enumerate(zip(sources, targets))]
    for copy in copies:
        copy.start()
    for copy in copies:
        copy.wait()
    row = lax.broadcasted_iota(jnp.int32, (8, ROWS), 0)
    lane = lax.broadcasted_iota(jnp.int32, (8, ROWS), 1)
    block = jnp.right_shift(pos_ref[...], 6).astype(jnp.float32)
    seg = seg_ref[...].astype(jnp.float32)
    tops = []
    for h in range(QH):
        cols = slice(h * HEAD, (h + 1) * HEAD)
        prod = g_ref[:, cols].astype(jnp.float32) * o_ref[:, cols].astype(jnp.float32)
        dot = jnp.sum(prod.T, axis=0, keepdims=True)
        lse = lse_ref[h : h + 1, :] * LOG2E
        tops.append(
            jnp.where(
                row == 0,
                lse,
                jnp.where(row == 1, dot, jnp.where(row == 2, block, jnp.where(row == 3, seg, 0.0))),
            )
        )
        for b in range(2):
            to = slice(h * BLOCK, (h + 1) * BLOCK)
            frm = slice(b * BLOCK, (b + 1) * BLOCK)
            qmsg_ref[b, to, 0:HEAD] = q_ref[frm, cols]
            qmsg_ref[b, to, HEAD : 2 * HEAD] = g_ref[frm, cols]
    for pair in range(2):
        first, second = tops[2 * pair], tops[2 * pair + 1]
        halves = (
            jnp.where(lane < BLOCK, first, pltpu.roll(second, BLOCK, 1)),
            jnp.where(lane < BLOCK, pltpu.roll(first, BLOCK, 1), second),
        )
        for b in range(2):
            full = halves[b]
            high = full.astype(jnp.bfloat16).astype(jnp.float32)
            middle = (full - high).astype(jnp.bfloat16).astype(jnp.float32)
            low = full - high - middle
            upper = jnp.where(row < 4, high, pltpu.roll(middle, 4, 0))
            lower = jnp.where(row < 4, low, 0.0)
            qmsg_ref[b, STACK : STACK + STATS, pair * ROWS : (pair + 1) * ROWS] = jnp.concatenate(
                [upper, lower], axis=0
            ).astype(jnp.bfloat16)
    tail = jnp.where(row == 0, block, jnp.where(row == 1, seg, 0.0))
    tail = jnp.concatenate([tail, jnp.zeros_like(tail)], axis=0).astype(jnp.bfloat16)
    for d in range(PLANE):
        kvmsg_ref[d, 0:ROWS, 0:HEAD] = k_ref[...]
        kvmsg_ref[d, 0:ROWS, HEAD : 2 * HEAD] = v_ref[...]
        kvmsg_ref[d, ROWS : ROWS + STATS, 0:ROWS] = tail
        kvmsg_ref[d, ROWS : ROWS + STATS, ROWS : 2 * ROWS] = jnp.zeros_like(tail)


def pack(queries, out_grad, saved_out, keys, values, log_sums, positions, segments):
    wide = pltpu.VMEM((ROWS, QH * HEAD), jnp.bfloat16)
    narrow = pltpu.VMEM((ROWS, HEAD), jnp.bfloat16)
    line = pltpu.VMEM((1, ROWS), jnp.int32)
    return pl.pallas_call(
        pack_kernel,
        out_shape=(
            jax.ShapeDtypeStruct((2, STACK + STATS, 2 * HEAD), jnp.bfloat16),
            jax.ShapeDtypeStruct((PLANE, ROWS + STATS, 2 * HEAD), jnp.bfloat16),
        ),
        in_specs=[pl.BlockSpec(memory_space=pl.ANY)] * 8,
        out_specs=(pl.BlockSpec(memory_space=pltpu.VMEM),) * 2,
        scratch_shapes=[
            wide,
            wide,
            wide,
            narrow,
            narrow,
            pltpu.VMEM((QH, ROWS), jnp.float32),
            line,
            line,
            pltpu.SemaphoreType.DMA((8,)),
        ],
        compiler_params=pltpu.CompilerParams(vmem_limit_bytes=8 * 1024 * 1024),
        name="pack",
    )(
        queries,
        out_grad,
        saved_out,
        keys,
        values,
        log_sums.T,
        positions.reshape(1, ROWS),
        segments.reshape(1, ROWS),
    )


def grad_kernel(*refs):
    q_refs = refs[:PIECES]
    (kv_ref, dkv_ref, own_ref, other_ref) = refs[PIECES : PIECES + 4]
    (qs, rows, dk, dv, dq, ints, ints_s, jobs, sem) = refs[PIECES + 4 :]
    scale = HEAD ** (-0.5)

    tails = [kv_ref[d, ROWS : ROWS + STATS, 0:ROWS].astype(jnp.float32) for d in range(PLANE)]
    number = jnp.concatenate([tail[0:1] for tail in tails], axis=0)
    key_seg = jnp.concatenate([tail[1:2] for tail in tails], axis=0)
    column = jnp.concatenate([number[:, 0:1], number[:, BLOCK : BLOCK + 1]], axis=0)
    column = jnp.broadcast_to(column, (KBLOCKS, ROWS))
    pad = jnp.full((ROWS - KBLOCKS, ROWS), FAR, jnp.float32)
    line = jnp.concatenate([column, pad], axis=0).T
    rank = jnp.sum((column < line[0:KBLOCKS]).astype(jnp.float32), axis=0, keepdims=True)
    slot = lax.broadcasted_iota(jnp.int32, (SLOTS, ROWS), 0).astype(jnp.float32)
    lane = lax.broadcasted_iota(jnp.int32, (SLOTS, ROWS), 1)
    order = jnp.sum(
        jnp.where((rank == slot) & (lane < KBLOCKS), lane.astype(jnp.float32), 0.0),
        axis=1,
        keepdims=True,
    )
    below = [
        jnp.sum((key_seg < float(s)).astype(jnp.float32), axis=0, keepdims=True) for s in range(1, 9)
    ]
    below = jnp.sum(jnp.concatenate(below, axis=0), axis=1, keepdims=True)
    below = jnp.broadcast_to(below, (8, STACK))
    segment = (lax.broadcasted_iota(jnp.int32, (8, STACK), 0) + 1).astype(jnp.float32)

    within = jnp.bitwise_and(lax.broadcasted_iota(jnp.int32, (1, STACK), 1), BLOCK - 1)
    within = within.astype(jnp.float32) + 1.0
    numbers, begins = [], []
    stats = []
    for qi in range(QBLOCKS):
        tail = q_refs[qi // 2][qi % 2, STACK : STACK + STATS, :].astype(jnp.float32)
        stat = tail[0:4] + tail[4:8] + tail[8:12]
        begin = jnp.max(jnp.where(stat[3:4] >= segment, below, 0.0), axis=0, keepdims=True)
        stats.append((stat, begin))
        numbers.append(stat[2:3, 0:1])
        begins.append(begin[:, 0:1])
    numbers = jnp.concatenate(numbers, axis=0)
    before = jnp.sum((line[0:QBLOCKS] < numbers).astype(jnp.float32), axis=1, keepdims=True)
    same = jnp.sum((line[0:QBLOCKS] == numbers).astype(jnp.float32), axis=1, keepdims=True)
    low = jnp.floor(jnp.concatenate(begins, axis=0) * (1.0 / BLOCK))
    empty = jnp.zeros((SLOTS - QBLOCKS, 1), jnp.float32)
    low = jnp.concatenate([low, empty], axis=0)
    high = jnp.concatenate([before + same, empty], axis=0)
    ints[...] = jnp.where(lane == 0, order, jnp.where(lane == 1, low, high)).astype(jnp.int32)
    copy = pltpu.make_async_copy(ints, ints_s, sem)
    copy.start()

    for qi in range(QBLOCKS):
        stat, begin = stats[qi]
        rows[qi, 0:1, :] = stat[0:1]
        rows[qi, 1:2, :] = stat[1:2]
        rows[qi, 2:3, :] = begin
        rows[qi, 3:4, :] = before[qi : qi + 1] * float(BLOCK) + same[qi : qi + 1] * within
        qs[qi] = q_refs[qi // 2][qi % 2, 0:STACK, :]
    dk[...] = jnp.zeros_like(dk)
    dv[...] = jnp.zeros_like(dv)
    dq[...] = jnp.zeros_like(dq)
    copy.wait()

    def list_block(qi, count):
        lower = ints_s[qi, 1]
        steps = jnp.right_shift(jnp.maximum(ints_s[qi, 2] - lower, 0) + (TILE_BLOCKS - 1), 2)

        def put(step, count):
            jobs[count] = qi * 64 + lower + step * TILE_BLOCKS
            return count + 1

        return lax.fori_loop(0, steps, put, count)

    count = lax.fori_loop(0, QBLOCKS, list_block, 0)
    jobs[count] = KBLOCKS
    down = lax.broadcasted_iota(jnp.int32, (TILE, ROWS), 0).astype(jnp.float32)
    nt = (((1,), (1,)), ((), ()))
    tn = (((0,), (0,)), ((), ()))

    def products(job):
        qi = jnp.right_shift(job, 6)
        at = jnp.bitwise_and(job, 63)
        blocks = [ints_s[at + i, 0] for i in range(TILE_BLOCKS)]
        kv = jnp.concatenate(
            [
                kv_ref[
                    jnp.bitwise_and(j, PLANE - 1),
                    pl.ds(pl.multiple_of(jnp.right_shift(j, 4) * BLOCK, BLOCK), BLOCK),
                    :,
                ]
                for j in blocks
            ],
            axis=0,
        )
        k, v = kv[:, 0:HEAD], kv[:, HEAD : 2 * HEAD]
        q, g = qs[qi, :, 0:HEAD], qs[qi, :, HEAD : 2 * HEAD]
        s = lax.dot_general(k, q, nt, preferred_element_type=jnp.float32)
        gp = lax.dot_general(v, g, nt, preferred_element_type=jnp.float32)
        offset = (at * BLOCK).astype(jnp.float32)
        begin = rows[qi, 2:3, 0:ROWS] - offset
        end = rows[qi, 3:4, 0:ROWS] - offset
        seen = (down >= begin) & (down < end)
        seen = jnp.concatenate([seen, seen], axis=1)
        w = jnp.where(seen, jnp.exp2(s * (scale * LOG2E) - rows[qi, 0:1, :]), 0.0)
        ds = (w * (gp - rows[qi, 1:2, :]) * scale).astype(jnp.bfloat16)
        dv_part = jnp.dot(w.astype(jnp.bfloat16), g, preferred_element_type=jnp.float32)
        dk_part = jnp.dot(ds, q, preferred_element_type=jnp.float32)
        dq_part = lax.dot_general(ds, k, tn, preferred_element_type=jnp.float32)
        return qi, blocks, dq_part, dk_part, dv_part

    def jobs_step(step, carry):
        done = [products(jobs[step * TOGETHER + i]) for i in range(TOGETHER)]
        for qi, blocks, dq_part, dk_part, dv_part in done:
            dq[qi] += dq_part
            for i, j in enumerate(blocks):
                part = slice(i * BLOCK, (i + 1) * BLOCK)
                dk[j] += dk_part[part]
                dv[j] += dv_part[part]
        return carry

    lax.fori_loop(0, jnp.right_shift(count + TOGETHER - 1, 1), jobs_step, 0)

    for j in range(KBLOCKS):
        d, to = j % PLANE, slice((j // PLANE) * BLOCK, (j // PLANE + 1) * BLOCK)
        dkv_ref[d, to, 0:HEAD] = dk[j].astype(jnp.bfloat16)
        dkv_ref[d, to, HEAD : 2 * HEAD] = dv[j].astype(jnp.bfloat16)
    for qi in range(QBLOCKS // 2):
        own_ref[qi] = dq[qi]
        other_ref[qi] = dq[QBLOCKS // 2 + qi].astype(jnp.bfloat16)


def grads(pieces, kv):
    half = QBLOCKS // 2
    return pl.pallas_call(
        grad_kernel,
        out_shape=(
            jax.ShapeDtypeStruct((PLANE, ROWS, 2 * HEAD), jnp.bfloat16),
            jax.ShapeDtypeStruct((half, STACK, HEAD), jnp.float32),
            jax.ShapeDtypeStruct((half, STACK, HEAD), jnp.bfloat16),
        ),
        in_specs=[pl.BlockSpec(memory_space=pltpu.VMEM)] * (PIECES + 1),
        out_specs=(pl.BlockSpec(memory_space=pltpu.VMEM),) * 3,
        scratch_shapes=[
            pltpu.VMEM((QBLOCKS, STACK, 2 * HEAD), jnp.bfloat16),
            pltpu.VMEM((QBLOCKS, 8, STACK), jnp.float32),
            pltpu.VMEM((KBLOCKS, BLOCK, HEAD), jnp.float32),
            pltpu.VMEM((KBLOCKS, BLOCK, HEAD), jnp.float32),
            pltpu.VMEM((QBLOCKS, STACK, HEAD), jnp.float32),
            pltpu.VMEM((SLOTS, ROWS), jnp.int32),
            pltpu.SMEM((SLOTS, ROWS), jnp.int32),
            pltpu.SMEM((QBLOCKS * KBLOCKS // TILE_BLOCKS + 8,), jnp.int32),
            pltpu.SemaphoreType.DMA,
        ],
        compiler_params=pltpu.CompilerParams(vmem_limit_bytes=16 * 1024 * 1024),
        name="grads",
    )(*pieces, kv)


def unstack(array):
    return array.reshape(2, QH, BLOCK, HEAD).transpose(0, 2, 1, 3).reshape(ROWS, QH * HEAD)


def body(queries, keys, values, saved_out, out_grad, log_sums, positions, segments):
    qmsg, kvmsg = pack(queries, out_grad, saved_out, keys, values, log_sums, positions, segments)
    column = [qmsg] + [along_z(qmsg, shift) for shift in (1, 2, 3)]
    kv = over_plane(kvmsg)
    column = column + [to_partner(piece) for piece in column]
    dkv, own, other = grads(column, kv)
    total = (own + to_partner(other).astype(jnp.float32)).reshape(DEPTH, 2, STACK, HEAD)
    back = [along_z(total[shift].astype(jnp.bfloat16), -shift) for shift in (1, 2, 3)]
    parts = over_plane(dkv)
    grad_kv = jnp.sum(parts.astype(jnp.float32), axis=0)
    grad_queries = total[0]
    for part in back:
        grad_queries = grad_queries + part.astype(jnp.float32)
    return (unstack(grad_queries), grad_kv[:, :HEAD], grad_kv[:, HEAD:])


def solution(mesh):
    rows2, rows1 = P(AXES, None), P(AXES)
    return jax.shard_map(
        body,
        mesh=mesh,
        in_specs=(rows2,) * 6 + (rows1,) * 2,
        out_specs=(rows2,) * 3,
        check_vma=False,
    )
```

```python
import math

import jax
import jax.numpy as jnp
from jax import lax
from jax.experimental import pallas as pl
from jax.experimental.pallas import tpu as pltpu
from jax.sharding import PartitionSpec as P

HEAD = 128
QH = 4
ROWS = 128
BLOCK = 64
STATS = 16
PLANE = 16
DEPTH = 4
PIECES = 2 * DEPTH
QBLOCKS = 2 * PIECES
KBLOCKS = 2 * PLANE
STACK = QH * BLOCK
TILE = 256
TILE_BLOCKS = TILE // BLOCK
SLOTS = 40
TOGETHER = 4
FAR = 1.0e9
AXES = ("outer", "inner")
LOG2E = math.log2(math.e)


def place(index):
    outer, inner = divmod(index, 32)
    return (inner // 16) * 2 + outer // 2, outer % 2, inner % 16


def index_of(z, core, spot):
    return ((z % 2) * 2 + core) * 32 + (z // 2) * 16 + spot


def along_z(array, shift):
    pairs = []
    for source in range(128):
        z, core, spot = place(source)
        pairs.append((source, index_of((z + shift) % DEPTH, core, spot)))
    return lax.ppermute(array, AXES, pairs)


def to_partner(array):
    pairs = []
    for source in range(128):
        z, core, spot = place(source)
        pairs.append((source, index_of(z, 1 - core, spot)))
    return lax.ppermute(array, AXES, pairs)


def over_plane(array):
    groups = [list(range(first, first + PLANE)) for first in (0, PLANE)]
    return lax.all_to_all(array, "inner", 0, 0, axis_index_groups=groups, tiled=True)


def pack_kernel(q_hbm, g_hbm, o_hbm, k_hbm, v_hbm, lse_hbm, pos_hbm, seg_hbm, qmsg_ref, kvmsg_ref, *scratch):
    (q_ref, g_ref, o_ref, k_ref, v_ref, lse_ref, pos_ref, seg_ref, sems) = scratch
    sources = (lse_hbm, pos_hbm, seg_hbm, g_hbm, o_hbm, q_hbm, k_hbm, v_hbm)
    targets = (lse_ref, pos_ref, seg_ref, g_ref, o_ref, q_ref, k_ref, v_ref)
    copies = [pltpu.make_async_copy(s, t, sems.at[i]) for i, (s, t) in enumerate(zip(sources, targets))]
    for copy in copies:
        copy.start()
    for copy in copies:
        copy.wait()
    row = lax.broadcasted_iota(jnp.int32, (8, ROWS), 0)
    lane = lax.broadcasted_iota(jnp.int32, (8, ROWS), 1)
    block = jnp.right_shift(pos_ref[...], 6).astype(jnp.float32)
    seg = seg_ref[...].astype(jnp.float32)
    tops = []
    for h in range(QH):
        cols = slice(h * HEAD, (h + 1) * HEAD)
        prod = g_ref[:, cols].astype(jnp.float32) * o_ref[:, cols].astype(jnp.float32)
        dot = jnp.sum(prod.T, axis=0, keepdims=True)
        lse = lse_ref[h : h + 1, :] * LOG2E
        tops.append(
            jnp.where(
                row == 0,
                lse,
                jnp.where(row == 1, dot, jnp.where(row == 2, block, jnp.where(row == 3, seg, 0.0))),
            )
        )
        for b in range(2):
            to = slice(h * BLOCK, (h + 1) * BLOCK)
            frm = slice(b * BLOCK, (b + 1) * BLOCK)
            qmsg_ref[b, to, 0:HEAD] = q_ref[frm, cols]
            qmsg_ref[b, to, HEAD : 2 * HEAD] = g_ref[frm, cols]
    for pair in range(2):
        first, second = tops[2 * pair], tops[2 * pair + 1]
        halves = (
            jnp.where(lane < BLOCK, first, pltpu.roll(second, BLOCK, 1)),
            jnp.where(lane < BLOCK, pltpu.roll(first, BLOCK, 1), second),
        )
        for b in range(2):
            full = halves[b]
            high = full.astype(jnp.bfloat16).astype(jnp.float32)
            middle = (full - high).astype(jnp.bfloat16).astype(jnp.float32)
            low = full - high - middle
            upper = jnp.where(row < 4, high, pltpu.roll(middle, 4, 0))
            lower = jnp.where(row < 4, low, 0.0)
            qmsg_ref[b, STACK : STACK + STATS, pair * ROWS : (pair + 1) * ROWS] = jnp.concatenate(
                [upper, lower], axis=0
            ).astype(jnp.bfloat16)
    tail = jnp.where(row == 0, block, jnp.where(row == 1, seg, 0.0))
    tail = jnp.concatenate([tail, jnp.zeros_like(tail)], axis=0).astype(jnp.bfloat16)
    for d in range(PLANE):
        kvmsg_ref[d, 0:ROWS, 0:HEAD] = k_ref[...]
        kvmsg_ref[d, 0:ROWS, HEAD : 2 * HEAD] = v_ref[...]
        kvmsg_ref[d, ROWS : ROWS + STATS, 0:ROWS] = tail
        kvmsg_ref[d, ROWS : ROWS + STATS, ROWS : 2 * ROWS] = jnp.zeros_like(tail)


def pack(queries, out_grad, saved_out, keys, values, log_sums, positions, segments):
    wide = pltpu.VMEM((ROWS, QH * HEAD), jnp.bfloat16)
    narrow = pltpu.VMEM((ROWS, HEAD), jnp.bfloat16)
    line = pltpu.VMEM((1, ROWS), jnp.int32)
    return pl.pallas_call(
        pack_kernel,
        out_shape=(
            jax.ShapeDtypeStruct((2, STACK + STATS, 2 * HEAD), jnp.bfloat16),
            jax.ShapeDtypeStruct((PLANE, ROWS + STATS, 2 * HEAD), jnp.bfloat16),
        ),
        in_specs=[pl.BlockSpec(memory_space=pltpu.HBM)] * 8,
        out_specs=(pl.BlockSpec(memory_space=pltpu.VMEM),) * 2,
        scratch_shapes=[
            wide,
            wide,
            wide,
            narrow,
            narrow,
            pltpu.VMEM((QH, ROWS), jnp.float32),
            line,
            line,
            pltpu.SemaphoreType.DMA((8,)),
        ],
        compiler_params=pltpu.CompilerParams(vmem_limit_bytes=8 * 1024 * 1024),
        name="pack",
    )(
        queries,
        out_grad,
        saved_out,
        keys,
        values,
        log_sums.T,
        positions.reshape(1, ROWS),
        segments.reshape(1, ROWS),
    )


def grad_kernel(*refs):
    q_refs = refs[:PIECES]
    (kv_ref, dkv_ref, own_ref, other_ref) = refs[PIECES : PIECES + 4]
    (qs, rows, dk, dv, dq, ints, ints_s, jobs, sem, q_sems) = refs[PIECES + 4 :]
    q_copies = [
        pltpu.make_async_copy(q_refs[p], qs.at[pl.ds(2 * p, 2)], q_sems.at[p]) for p in range(PIECES)
    ]
    for copy in q_copies:
        copy.start()
    dk[...] = jnp.zeros_like(dk)
    dv[...] = jnp.zeros_like(dv)
    dq[...] = jnp.zeros_like(dq)
    scale = HEAD ** (-0.5)

    tails = [kv_ref[d, ROWS : ROWS + STATS, 0:ROWS].astype(jnp.float32) for d in range(PLANE)]
    number = jnp.concatenate([tail[0:1] for tail in tails], axis=0)
    key_seg = jnp.concatenate([tail[1:2] for tail in tails], axis=0)
    column = jnp.concatenate([number[:, 0:1], number[:, BLOCK : BLOCK + 1]], axis=0)
    column = jnp.broadcast_to(column, (KBLOCKS, ROWS))
    pad = jnp.full((ROWS - KBLOCKS, ROWS), FAR, jnp.float32)
    line = jnp.concatenate([column, pad], axis=0).T
    rank = jnp.sum((column < line[0:KBLOCKS]).astype(jnp.float32), axis=0, keepdims=True)
    slot = lax.broadcasted_iota(jnp.int32, (SLOTS, ROWS), 0).astype(jnp.float32)
    lane = lax.broadcasted_iota(jnp.int32, (SLOTS, ROWS), 1)
    order = jnp.sum(
        jnp.where((rank == slot) & (lane < KBLOCKS), lane.astype(jnp.float32), 0.0),
        axis=1,
        keepdims=True,
    )
    below = [
        jnp.sum((key_seg < float(s)).astype(jnp.float32), axis=0, keepdims=True) for s in range(1, 9)
    ]
    below = jnp.sum(jnp.concatenate(below, axis=0), axis=1, keepdims=True)
    below = jnp.broadcast_to(below, (8, STACK))
    segment = (lax.broadcasted_iota(jnp.int32, (8, STACK), 0) + 1).astype(jnp.float32)

    within = jnp.bitwise_and(lax.broadcasted_iota(jnp.int32, (1, STACK), 1), BLOCK - 1)
    within = within.astype(jnp.float32) + 1.0
    numbers, begins = [], []
    stats = []
    for qi in range(QBLOCKS):
        if qi % 2 == 0:
            q_copies[qi // 2].wait()
        tail = qs[qi, STACK : STACK + STATS, :].astype(jnp.float32)
        stat = tail[0:4] + tail[4:8] + tail[8:12]
        begin = jnp.max(jnp.where(stat[3:4] >= segment, below, 0.0), axis=0, keepdims=True)
        stats.append((stat, begin))
        numbers.append(stat[2:3, 0:1])
        begins.append(begin[:, 0:1])
    numbers = jnp.concatenate(numbers, axis=0)
    before = jnp.sum((line[0:QBLOCKS] < numbers).astype(jnp.float32), axis=1, keepdims=True)
    same = jnp.sum((line[0:QBLOCKS] == numbers).astype(jnp.float32), axis=1, keepdims=True)
    low = jnp.floor(jnp.concatenate(begins, axis=0) * (1.0 / BLOCK))
    empty = jnp.zeros((SLOTS - QBLOCKS, 1), jnp.float32)
    low = jnp.concatenate([low, empty], axis=0)
    high = jnp.concatenate([before + same, empty], axis=0)
    ints[...] = jnp.where(lane == 0, order, jnp.where(lane == 1, low, high)).astype(jnp.int32)
    copy = pltpu.make_async_copy(ints, ints_s, sem)
    copy.start()

    for qi in range(QBLOCKS):
        stat, begin = stats[qi]
        rows[qi, 0:1, :] = stat[0:1]
        rows[qi, 1:2, :] = stat[1:2]
        rows[qi, 2:3, :] = begin
        rows[qi, 3:4, :] = before[qi : qi + 1] * float(BLOCK) + same[qi : qi + 1] * within
    copy.wait()

    def list_block(qi, count):
        lower = ints_s[qi, 1]
        steps = jnp.right_shift(jnp.maximum(ints_s[qi, 2] - lower, 0) + (TILE_BLOCKS - 1), 2)

        def put(step, count):
            jobs[count] = qi * 64 + lower + step * TILE_BLOCKS
            return count + 1

        return lax.fori_loop(0, steps, put, count)

    count = lax.fori_loop(0, QBLOCKS, list_block, 0)
    for i in range(TOGETHER - 1):
        jobs[count + i] = KBLOCKS
    down = lax.broadcasted_iota(jnp.int32, (TILE, ROWS), 0).astype(jnp.float32)
    nt = (((1,), (1,)), ((), ()))
    tn = (((0,), (0,)), ((), ()))

    def products(job):
        qi = jnp.right_shift(job, 6)
        at = jnp.bitwise_and(job, 63)
        blocks = [ints_s[at + i, 0] for i in range(TILE_BLOCKS)]
        kv = jnp.concatenate(
            [
                kv_ref[
                    jnp.bitwise_and(j, PLANE - 1),
                    pl.ds(pl.multiple_of(jnp.right_shift(j, 4) * BLOCK, BLOCK), BLOCK),
                    :,
                ]
                for j in blocks
            ],
            axis=0,
        )
        k, v = kv[:, 0:HEAD], kv[:, HEAD : 2 * HEAD]
        q, g = qs[qi, 0:STACK, 0:HEAD], qs[qi, 0:STACK, HEAD : 2 * HEAD]
        s = lax.dot_general(k, q, nt, preferred_element_type=jnp.float32)
        gp = lax.dot_general(v, g, nt, preferred_element_type=jnp.float32)
        offset = (at * BLOCK).astype(jnp.float32)
        begin = rows[qi, 2:3, 0:ROWS] - offset
        end = rows[qi, 3:4, 0:ROWS] - offset
        seen = (down >= begin) & (down < end)
        seen = jnp.concatenate([seen, seen], axis=1)
        w = jnp.where(seen, jnp.exp2(s * (scale * LOG2E) - rows[qi, 0:1, :]), 0.0)
        ds = (w * (gp - rows[qi, 1:2, :]) * scale).astype(jnp.bfloat16)
        dv_part = jnp.dot(w.astype(jnp.bfloat16), g, preferred_element_type=jnp.float32)
        dk_part = jnp.dot(ds, q, preferred_element_type=jnp.float32)
        dq_part = lax.dot_general(k, ds, tn, preferred_element_type=jnp.float32)
        return qi, blocks, dq_part, dk_part, dv_part

    def jobs_step(step, carry):
        done = [products(jobs[step * TOGETHER + i]) for i in range(TOGETHER)]
        for qi, blocks, dq_part, dk_part, dv_part in done:
            dq[qi] += dq_part
            for i, j in enumerate(blocks):
                part = slice(i * BLOCK, (i + 1) * BLOCK)
                dk[j] += dk_part[part]
                dv[j] += dv_part[part]
        return carry

    lax.fori_loop(0, jnp.right_shift(count + TOGETHER - 1, 2), jobs_step, 0)

    for j in range(KBLOCKS):
        d, to = j % PLANE, slice((j // PLANE) * BLOCK, (j // PLANE + 1) * BLOCK)
        dkv_ref[d, to, 0:HEAD] = dk[j].astype(jnp.bfloat16)
        dkv_ref[d, to, HEAD : 2 * HEAD] = dv[j].astype(jnp.bfloat16)
    for qi in range(QBLOCKS // 2):
        own_ref[qi] = dq[qi].T
        other_ref[qi] = dq[QBLOCKS // 2 + qi].T.astype(jnp.bfloat16)


def grads(pieces, kv):
    half = QBLOCKS // 2
    return pl.pallas_call(
        grad_kernel,
        out_shape=(
            jax.ShapeDtypeStruct((PLANE, ROWS, 2 * HEAD), jnp.bfloat16),
            jax.ShapeDtypeStruct((half, STACK, HEAD), jnp.float32),
            jax.ShapeDtypeStruct((half, STACK, HEAD), jnp.bfloat16),
        ),
        in_specs=[pl.BlockSpec(memory_space=pltpu.HBM)] * PIECES
        + [pl.BlockSpec(memory_space=pltpu.VMEM)],
        out_specs=(pl.BlockSpec(memory_space=pltpu.VMEM),) * 3,
        scratch_shapes=[
            pltpu.VMEM((QBLOCKS, STACK + STATS, 2 * HEAD), jnp.bfloat16),
            pltpu.VMEM((QBLOCKS, 8, STACK), jnp.float32),
            pltpu.VMEM((KBLOCKS, BLOCK, HEAD), jnp.float32),
            pltpu.VMEM((KBLOCKS, BLOCK, HEAD), jnp.float32),
            pltpu.VMEM((QBLOCKS, HEAD, STACK), jnp.float32),
            pltpu.VMEM((SLOTS, ROWS), jnp.int32),
            pltpu.SMEM((SLOTS, ROWS), jnp.int32),
            pltpu.SMEM((QBLOCKS * KBLOCKS // TILE_BLOCKS + 8,), jnp.int32),
            pltpu.SemaphoreType.DMA,
            pltpu.SemaphoreType.DMA((PIECES,)),
        ],
        compiler_params=pltpu.CompilerParams(vmem_limit_bytes=16 * 1024 * 1024),
        name="grads",
    )(*pieces, kv)


def unstack(array):
    return array.reshape(2, QH, BLOCK, HEAD).transpose(0, 2, 1, 3).reshape(ROWS, QH * HEAD)


def body(queries, keys, values, saved_out, out_grad, log_sums, positions, segments):
    qmsg, kvmsg = pack(queries, out_grad, saved_out, keys, values, log_sums, positions, segments)
    column = [qmsg] + [along_z(qmsg, shift) for shift in (1, 2, 3)]
    kv = over_plane(kvmsg)
    column = column + [to_partner(piece) for piece in column]
    dkv, own, other = grads(column, kv)
    total = (own + to_partner(other).astype(jnp.float32)).reshape(DEPTH, 2, STACK, HEAD)
    back = [along_z(total[shift].astype(jnp.bfloat16), -shift) for shift in (1, 2, 3)]
    parts = over_plane(dkv)
    grad_kv = jnp.sum(parts.astype(jnp.float32), axis=0)
    grad_queries = total[0]
    for part in back:
        grad_queries = grad_queries + part.astype(jnp.float32)
    return (unstack(grad_queries), grad_kv[:, :HEAD], grad_kv[:, HEAD:])


def solution(mesh):
    rows2, rows1 = P(AXES, None), P(AXES)
    return jax.shard_map(
        body,
        mesh=mesh,
        in_specs=(rows2,) * 6 + (rows1,) * 2,
        out_specs=(rows2,) * 3,
        check_vma=False,
    )
```

```python
import math

import jax
import jax.numpy as jnp
from jax import lax
from jax.experimental import pallas as pl
from jax.experimental.pallas import tpu as pltpu
from jax.sharding import PartitionSpec as P

HEAD = 128
QH = 4
ROWS = 128
BLOCK = 64
STATS = 16
PLANE = 16
DEPTH = 4
PIECES = 2 * DEPTH
QBLOCKS = 2 * PIECES
KBLOCKS = 2 * PLANE
STACK = QH * BLOCK
TILE = 256
TILE_BLOCKS = TILE // BLOCK
SLOTS = 40
TOGETHER = 4
FAR = 1.0e9
AXES = ("outer", "inner")
LOG2E = math.log2(math.e)


def place(index):
    outer, inner = divmod(index, 32)
    return (inner // 16) * 2 + outer // 2, outer % 2, inner % 16


def index_of(z, core, spot):
    return ((z % 2) * 2 + core) * 32 + (z // 2) * 16 + spot


def along_z(array, shift):
    pairs = []
    for source in range(128):
        z, core, spot = place(source)
        pairs.append((source, index_of((z + shift) % DEPTH, core, spot)))
    return lax.ppermute(array, AXES, pairs)


def to_partner(array):
    pairs = []
    for source in range(128):
        z, core, spot = place(source)
        pairs.append((source, index_of(z, 1 - core, spot)))
    return lax.ppermute(array, AXES, pairs)


def over_plane(array):
    groups = [list(range(first, first + PLANE)) for first in (0, PLANE)]
    return lax.all_to_all(array, "inner", 0, 0, axis_index_groups=groups, tiled=True)


def pack_kernel(q_hbm, g_hbm, o_hbm, k_hbm, v_hbm, lse_hbm, pos_hbm, seg_hbm, qmsg_ref, kvmsg_ref, *scratch):
    (q_ref, g_ref, o_ref, k_ref, v_ref, lse_ref, pos_ref, seg_ref, sems) = scratch
    sources = (lse_hbm, pos_hbm, seg_hbm, g_hbm, o_hbm, q_hbm, k_hbm, v_hbm)
    targets = (lse_ref, pos_ref, seg_ref, g_ref, o_ref, q_ref, k_ref, v_ref)
    copies = [pltpu.make_async_copy(s, t, sems.at[i]) for i, (s, t) in enumerate(zip(sources, targets))]
    for copy in copies:
        copy.start()
    for copy in copies:
        copy.wait()
    row = lax.broadcasted_iota(jnp.int32, (8, ROWS), 0)
    lane = lax.broadcasted_iota(jnp.int32, (8, ROWS), 1)
    block = jnp.right_shift(pos_ref[...], 6).astype(jnp.float32)
    seg = seg_ref[...].astype(jnp.float32)
    tops = []
    for h in range(QH):
        cols = slice(h * HEAD, (h + 1) * HEAD)
        prod = g_ref[:, cols].astype(jnp.float32) * o_ref[:, cols].astype(jnp.float32)
        dot = jnp.sum(prod.T, axis=0, keepdims=True)
        lse = lse_ref[h : h + 1, :] * LOG2E
        tops.append(
            jnp.where(
                row == 0,
                lse,
                jnp.where(row == 1, dot, jnp.where(row == 2, block, jnp.where(row == 3, seg, 0.0))),
            )
        )
        for b in range(2):
            to = slice(h * BLOCK, (h + 1) * BLOCK)
            frm = slice(b * BLOCK, (b + 1) * BLOCK)
            qmsg_ref[b, to, 0:HEAD] = q_ref[frm, cols]
            qmsg_ref[b, to, HEAD : 2 * HEAD] = g_ref[frm, cols]
    for pair in range(2):
        first, second = tops[2 * pair], tops[2 * pair + 1]
        halves = (
            jnp.where(lane < BLOCK, first, pltpu.roll(second, BLOCK, 1)),
            jnp.where(lane < BLOCK, pltpu.roll(first, BLOCK, 1), second),
        )
        for b in range(2):
            full = halves[b]
            high = full.astype(jnp.bfloat16).astype(jnp.float32)
            middle = (full - high).astype(jnp.bfloat16).astype(jnp.float32)
            low = full - high - middle
            upper = jnp.where(row < 4, high, pltpu.roll(middle, 4, 0))
            lower = jnp.where(row < 4, low, 0.0)
            qmsg_ref[b, STACK : STACK + STATS, pair * ROWS : (pair + 1) * ROWS] = jnp.concatenate(
                [upper, lower], axis=0
            ).astype(jnp.bfloat16)
    tail = jnp.where(row == 0, block, jnp.where(row == 1, seg, 0.0))
    tail = jnp.concatenate([tail, jnp.zeros_like(tail)], axis=0).astype(jnp.bfloat16)
    for d in range(PLANE):
        kvmsg_ref[d, 0:ROWS, 0:HEAD] = k_ref[...]
        kvmsg_ref[d, 0:ROWS, HEAD : 2 * HEAD] = v_ref[...]
        kvmsg_ref[d, ROWS : ROWS + STATS, 0:ROWS] = tail
        kvmsg_ref[d, ROWS : ROWS + STATS, ROWS : 2 * ROWS] = jnp.zeros_like(tail)


def pack(queries, out_grad, saved_out, keys, values, log_sums, positions, segments):
    wide = pltpu.VMEM((ROWS, QH * HEAD), jnp.bfloat16)
    narrow = pltpu.VMEM((ROWS, HEAD), jnp.bfloat16)
    line = pltpu.VMEM((1, ROWS), jnp.int32)
    return pl.pallas_call(
        pack_kernel,
        out_shape=(
            jax.ShapeDtypeStruct((2, STACK + STATS, 2 * HEAD), jnp.bfloat16),
            jax.ShapeDtypeStruct((PLANE, ROWS + STATS, 2 * HEAD), jnp.bfloat16),
        ),
        in_specs=[pl.BlockSpec(memory_space=pltpu.HBM)] * 8,
        out_specs=(pl.BlockSpec(memory_space=pltpu.VMEM),) * 2,
        scratch_shapes=[
            wide,
            wide,
            wide,
            narrow,
            narrow,
            pltpu.VMEM((QH, ROWS), jnp.float32),
            line,
            line,
            pltpu.SemaphoreType.DMA((8,)),
        ],
        compiler_params=pltpu.CompilerParams(vmem_limit_bytes=56 * 1024 * 1024),
        name="pack",
    )(
        queries,
        out_grad,
        saved_out,
        keys,
        values,
        log_sums.T,
        positions.reshape(1, ROWS),
        segments.reshape(1, ROWS),
    )


def grad_kernel(*refs):
    q_refs = refs[:PIECES]
    (kv_ref, dkv_ref, own_ref, other_ref) = refs[PIECES : PIECES + 4]
    (qs, rows, dk, dv, dq, ints, ints_s, jobs, sem, q_sems) = refs[PIECES + 4 :]
    q_copies = [
        pltpu.make_async_copy(q_refs[p], qs.at[pl.ds(2 * p, 2)], q_sems.at[p]) for p in range(PIECES)
    ]
    for copy in q_copies:
        copy.start()
    dk[...] = jnp.zeros_like(dk)
    dv[...] = jnp.zeros_like(dv)
    dq[...] = jnp.zeros_like(dq)
    scale = HEAD ** (-0.5)

    tails = [kv_ref[d, ROWS : ROWS + STATS, 0:ROWS].astype(jnp.float32) for d in range(PLANE)]
    number = jnp.concatenate([tail[0:1] for tail in tails], axis=0)
    key_seg = jnp.concatenate([tail[1:2] for tail in tails], axis=0)
    column = jnp.concatenate([number[:, 0:1], number[:, BLOCK : BLOCK + 1]], axis=0)
    column = jnp.broadcast_to(column, (KBLOCKS, ROWS))
    pad = jnp.full((ROWS - KBLOCKS, ROWS), FAR, jnp.float32)
    line = jnp.concatenate([column, pad], axis=0).T
    rank = jnp.sum((column < line[0:KBLOCKS]).astype(jnp.float32), axis=0, keepdims=True)
    slot = lax.broadcasted_iota(jnp.int32, (SLOTS, ROWS), 0).astype(jnp.float32)
    lane = lax.broadcasted_iota(jnp.int32, (SLOTS, ROWS), 1)
    order = jnp.sum(
        jnp.where((rank == slot) & (lane < KBLOCKS), lane.astype(jnp.float32), 0.0),
        axis=1,
        keepdims=True,
    )
    below = [
        jnp.sum((key_seg < float(s)).astype(jnp.float32), axis=0, keepdims=True) for s in range(1, 9)
    ]
    below = jnp.sum(jnp.concatenate(below, axis=0), axis=1, keepdims=True)
    below = jnp.broadcast_to(below, (8, STACK))
    segment = (lax.broadcasted_iota(jnp.int32, (8, STACK), 0) + 1).astype(jnp.float32)

    within = jnp.bitwise_and(lax.broadcasted_iota(jnp.int32, (1, STACK), 1), BLOCK - 1)
    within = within.astype(jnp.float32) + 1.0
    numbers, begins = [], []
    stats = []
    for qi in range(QBLOCKS):
        if qi % 2 == 0:
            q_copies[qi // 2].wait()
        tail = qs[qi, STACK : STACK + STATS, :].astype(jnp.float32)
        stat = tail[0:4] + tail[4:8] + tail[8:12]
        begin = jnp.max(jnp.where(stat[3:4] >= segment, below, 0.0), axis=0, keepdims=True)
        stats.append((stat, begin))
        numbers.append(stat[2:3, 0:1])
        begins.append(begin[:, 0:1])
    numbers = jnp.concatenate(numbers, axis=0)
    before = jnp.sum((line[0:QBLOCKS] < numbers).astype(jnp.float32), axis=1, keepdims=True)
    same = jnp.sum((line[0:QBLOCKS] == numbers).astype(jnp.float32), axis=1, keepdims=True)
    low = jnp.floor(jnp.concatenate(begins, axis=0) * (1.0 / BLOCK))
    empty = jnp.zeros((SLOTS - QBLOCKS, 1), jnp.float32)
    low = jnp.concatenate([low, empty], axis=0)
    high = jnp.concatenate([before + same, empty], axis=0)
    ints[...] = jnp.where(lane == 0, order, jnp.where(lane == 1, low, high)).astype(jnp.int32)
    copy = pltpu.make_async_copy(ints, ints_s, sem)
    copy.start()

    for qi in range(QBLOCKS):
        stat, begin = stats[qi]
        rows[qi, 0:1, :] = stat[0:1]
        rows[qi, 1:2, :] = stat[1:2]
        rows[qi, 2:3, :] = begin
        rows[qi, 3:4, :] = before[qi : qi + 1] * float(BLOCK) + same[qi : qi + 1] * within
    copy.wait()

    def list_block(qi, count):
        lower = ints_s[qi, 1]
        steps = jnp.right_shift(jnp.maximum(ints_s[qi, 2] - lower, 0) + (TILE_BLOCKS - 1), 2)

        def put(step, count):
            jobs[count] = qi * 64 + lower + step * TILE_BLOCKS
            return count + 1

        return lax.fori_loop(0, steps, put, count)

    count = lax.fori_loop(0, QBLOCKS, list_block, 0)
    for i in range(TOGETHER - 1):
        jobs[count + i] = KBLOCKS
    down = lax.broadcasted_iota(jnp.int32, (TILE, ROWS), 0).astype(jnp.float32)
    nt = (((1,), (1,)), ((), ()))
    tn = (((0,), (0,)), ((), ()))

    def products(job):
        qi = jnp.right_shift(job, 6)
        at = jnp.bitwise_and(job, 63)
        blocks = [ints_s[at + i, 0] for i in range(TILE_BLOCKS)]
        kv = jnp.concatenate(
            [
                kv_ref[
                    jnp.bitwise_and(j, PLANE - 1),
                    pl.ds(pl.multiple_of(jnp.right_shift(j, 4) * BLOCK, BLOCK), BLOCK),
                    :,
                ]
                for j in blocks
            ],
            axis=0,
        )
        k, v = kv[:, 0:HEAD], kv[:, HEAD : 2 * HEAD]
        q, g = qs[qi, 0:STACK, 0:HEAD], qs[qi, 0:STACK, HEAD : 2 * HEAD]
        s = lax.dot_general(k, q, nt, preferred_element_type=jnp.float32)
        gp = lax.dot_general(v, g, nt, preferred_element_type=jnp.float32)
        offset = (at * BLOCK).astype(jnp.float32)
        begin = rows[qi, 2:3, 0:ROWS] - offset
        end = rows[qi, 3:4, 0:ROWS] - offset
        seen = (down >= begin) & (down < end)
        seen = jnp.concatenate([seen, seen], axis=1)
        w = jnp.where(seen, jnp.exp2(s * (scale * LOG2E) - rows[qi, 0:1, :]), 0.0)
        ds = (w * (gp - rows[qi, 1:2, :]) * scale).astype(jnp.bfloat16)
        dv_part = jnp.dot(w.astype(jnp.bfloat16), g, preferred_element_type=jnp.float32)
        dk_part = jnp.dot(ds, q, preferred_element_type=jnp.float32)
        dq_part = lax.dot_general(k, ds, tn, preferred_element_type=jnp.float32)
        return qi, blocks, dq_part, dk_part, dv_part

    def jobs_step(step, carry):
        done = [products(jobs[step * TOGETHER + i]) for i in range(TOGETHER)]
        for qi, blocks, dq_part, dk_part, dv_part in done:
            dq[qi] += dq_part
            for i, j in enumerate(blocks):
                part = slice(i * BLOCK, (i + 1) * BLOCK)
                dk[j] += dk_part[part]
                dv[j] += dv_part[part]
        return carry

    lax.fori_loop(0, jnp.right_shift(count + TOGETHER - 1, 2), jobs_step, 0)

    for j in range(KBLOCKS):
        d, to = j % PLANE, slice((j // PLANE) * BLOCK, (j // PLANE + 1) * BLOCK)
        dkv_ref[d, to, 0:HEAD] = dk[j].astype(jnp.bfloat16)
        dkv_ref[d, to, HEAD : 2 * HEAD] = dv[j].astype(jnp.bfloat16)
    for qi in range(QBLOCKS // 2):
        own_ref[qi] = dq[qi].T
        other_ref[qi] = dq[QBLOCKS // 2 + qi].T.astype(jnp.bfloat16)


def grads(pieces, kv):
    half = QBLOCKS // 2
    return pl.pallas_call(
        grad_kernel,
        out_shape=(
            jax.ShapeDtypeStruct((PLANE, ROWS, 2 * HEAD), jnp.bfloat16),
            jax.ShapeDtypeStruct((half, STACK, HEAD), jnp.float32),
            jax.ShapeDtypeStruct((half, STACK, HEAD), jnp.bfloat16),
        ),
        in_specs=[pl.BlockSpec(memory_space=pltpu.HBM)] * PIECES
        + [pl.BlockSpec(memory_space=pltpu.VMEM)],
        out_specs=(pl.BlockSpec(memory_space=pltpu.VMEM),) * 3,
        scratch_shapes=[
            pltpu.VMEM((QBLOCKS, STACK + STATS, 2 * HEAD), jnp.bfloat16),
            pltpu.VMEM((QBLOCKS, 8, STACK), jnp.float32),
            pltpu.VMEM((KBLOCKS, BLOCK, HEAD), jnp.float32),
            pltpu.VMEM((KBLOCKS, BLOCK, HEAD), jnp.float32),
            pltpu.VMEM((QBLOCKS, HEAD, STACK), jnp.float32),
            pltpu.VMEM((SLOTS, ROWS), jnp.int32),
            pltpu.SMEM((SLOTS, ROWS), jnp.int32),
            pltpu.SMEM((QBLOCKS * KBLOCKS // TILE_BLOCKS + 8,), jnp.int32),
            pltpu.SemaphoreType.DMA,
            pltpu.SemaphoreType.DMA((PIECES,)),
        ],
        compiler_params=pltpu.CompilerParams(vmem_limit_bytes=50 * 1024 * 1024),
        name="grads",
    )(*pieces, kv)


def unstack(array):
    return array.reshape(2, QH, BLOCK, HEAD).transpose(0, 2, 1, 3).reshape(ROWS, QH * HEAD)


def body(queries, keys, values, saved_out, out_grad, log_sums, positions, segments):
    qmsg, kvmsg = pack(queries, out_grad, saved_out, keys, values, log_sums, positions, segments)
    column = [qmsg] + [along_z(qmsg, shift) for shift in (1, 2, 3)]
    kv = over_plane(kvmsg)
    column = column + [to_partner(piece) for piece in column]
    dkv, own, other = grads(column, kv)
    total = (own + to_partner(other).astype(jnp.float32)).reshape(DEPTH, 2, STACK, HEAD)
    back = [along_z(total[shift].astype(jnp.bfloat16), -shift) for shift in (1, 2, 3)]
    parts = over_plane(dkv)
    grad_keys = jnp.sum(parts[:, :, :HEAD].astype(jnp.float32), axis=0)
    grad_values = jnp.sum(parts[:, :, HEAD:].astype(jnp.float32), axis=0)
    grad_queries = total[0]
    for part in back:
        grad_queries = grad_queries + part.astype(jnp.float32)
    return (unstack(grad_queries), grad_keys, grad_values)


def solution(mesh):
    rows2, rows1 = P(AXES, None), P(AXES)
    return jax.shard_map(
        body,
        mesh=mesh,
        in_specs=(rows2,) * 6 + (rows1,) * 2,
        out_specs=(rows2,) * 3,
        check_vma=False,
    )
```

```python
import math

import jax
import jax.numpy as jnp
from jax import lax
from jax.experimental import pallas as pl
from jax.experimental.pallas import tpu as pltpu
from jax.sharding import PartitionSpec as P

HEAD = 128
QH = 4
ROWS = 128
BLOCK = 64
STATS = 16
PLANE = 16
DEPTH = 4
PIECES = 2 * DEPTH
QBLOCKS = 2 * PIECES
KBLOCKS = 2 * PLANE
STACK = QH * BLOCK
TILE = 256
TILE_BLOCKS = TILE // BLOCK
JOBS = 256
TOGETHER = 6
FAR = 1.0e9
AXES = ("outer", "inner")
LOG2E = math.log2(math.e)


def place(index):
    outer, inner = divmod(index, 32)
    return (inner // 16) * 2 + outer // 2, outer % 2, inner % 16


def index_of(z, core, spot):
    return ((z % 2) * 2 + core) * 32 + (z // 2) * 16 + spot


def along_z(array, shift):
    pairs = []
    for source in range(128):
        z, core, spot = place(source)
        pairs.append((source, index_of((z + shift) % DEPTH, core, spot)))
    return lax.ppermute(array, AXES, pairs)


def to_partner(array):
    pairs = []
    for source in range(128):
        z, core, spot = place(source)
        pairs.append((source, index_of(z, 1 - core, spot)))
    return lax.ppermute(array, AXES, pairs)


def over_plane(array):
    groups = [list(range(first, first + PLANE)) for first in (0, PLANE)]
    return lax.all_to_all(array, "inner", 0, 0, axis_index_groups=groups, tiled=True)


def pack_kernel(q_hbm, g_hbm, o_hbm, k_hbm, v_hbm, lse_hbm, pos_hbm, seg_hbm, qmsg_ref, kvmsg_ref, *scratch):
    (q_ref, g_ref, o_ref, k_ref, v_ref, lse_ref, pos_ref, seg_ref, sems) = scratch
    sources = (lse_hbm, pos_hbm, seg_hbm, g_hbm, o_hbm, q_hbm, k_hbm, v_hbm)
    targets = (lse_ref, pos_ref, seg_ref, g_ref, o_ref, q_ref, k_ref, v_ref)
    copies = [pltpu.make_async_copy(s, t, sems.at[i]) for i, (s, t) in enumerate(zip(sources, targets))]
    for copy in copies:
        copy.start()
    for copy in copies:
        copy.wait()
    row = lax.broadcasted_iota(jnp.int32, (8, ROWS), 0)
    lane = lax.broadcasted_iota(jnp.int32, (8, ROWS), 1)
    block = jnp.right_shift(pos_ref[...], 6).astype(jnp.float32)
    seg = seg_ref[...].astype(jnp.float32)
    tops = []
    for h in range(QH):
        cols = slice(h * HEAD, (h + 1) * HEAD)
        prod = g_ref[:, cols].astype(jnp.float32) * o_ref[:, cols].astype(jnp.float32)
        dot = jnp.sum(prod.T, axis=0, keepdims=True)
        lse = lse_ref[h : h + 1, :] * LOG2E
        tops.append(
            jnp.where(
                row == 0,
                lse,
                jnp.where(row == 1, dot, jnp.where(row == 2, block, jnp.where(row == 3, seg, 0.0))),
            )
        )
        for b in range(2):
            to = slice(h * BLOCK, (h + 1) * BLOCK)
            frm = slice(b * BLOCK, (b + 1) * BLOCK)
            qmsg_ref[b, to, 0:HEAD] = q_ref[frm, cols]
            qmsg_ref[b, to, HEAD : 2 * HEAD] = g_ref[frm, cols]
    for pair in range(2):
        first, second = tops[2 * pair], tops[2 * pair + 1]
        halves = (
            jnp.where(lane < BLOCK, first, pltpu.roll(second, BLOCK, 1)),
            jnp.where(lane < BLOCK, pltpu.roll(first, BLOCK, 1), second),
        )
        for b in range(2):
            full = halves[b]
            high = full.astype(jnp.bfloat16).astype(jnp.float32)
            middle = (full - high).astype(jnp.bfloat16).astype(jnp.float32)
            low = full - high - middle
            upper = jnp.where(row < 4, high, pltpu.roll(middle, 4, 0))
            lower = jnp.where(row < 4, low, 0.0)
            qmsg_ref[b, STACK : STACK + STATS, pair * ROWS : (pair + 1) * ROWS] = jnp.concatenate(
                [upper, lower], axis=0
            ).astype(jnp.bfloat16)
    tail = jnp.where(row == 0, block, jnp.where(row == 1, seg, 0.0))
    tail = jnp.concatenate([tail, jnp.zeros_like(tail)], axis=0).astype(jnp.bfloat16)
    for d in range(PLANE):
        kvmsg_ref[d, 0:ROWS, 0:HEAD] = k_ref[...]
        kvmsg_ref[d, 0:ROWS, HEAD : 2 * HEAD] = v_ref[...]
        kvmsg_ref[d, ROWS : ROWS + STATS, 0:ROWS] = tail
        kvmsg_ref[d, ROWS : ROWS + STATS, ROWS : 2 * ROWS] = jnp.zeros_like(tail)


def pack(queries, out_grad, saved_out, keys, values, log_sums, positions, segments):
    wide = pltpu.VMEM((ROWS, QH * HEAD), jnp.bfloat16)
    narrow = pltpu.VMEM((ROWS, HEAD), jnp.bfloat16)
    line = pltpu.VMEM((1, ROWS), jnp.int32)
    return pl.pallas_call(
        pack_kernel,
        out_shape=(
            jax.ShapeDtypeStruct((2, STACK + STATS, 2 * HEAD), jnp.bfloat16),
            jax.ShapeDtypeStruct((PLANE, ROWS + STATS, 2 * HEAD), jnp.bfloat16),
        ),
        in_specs=[pl.BlockSpec(memory_space=pltpu.HBM)] * 8,
        out_specs=(pl.BlockSpec(memory_space=pltpu.VMEM),) * 2,
        scratch_shapes=[
            wide,
            wide,
            wide,
            narrow,
            narrow,
            pltpu.VMEM((QH, ROWS), jnp.float32),
            line,
            line,
            pltpu.SemaphoreType.DMA((8,)),
        ],
        compiler_params=pltpu.CompilerParams(vmem_limit_bytes=56 * 1024 * 1024),
        name="pack",
    )(
        queries,
        out_grad,
        saved_out,
        keys,
        values,
        log_sums.T,
        positions.reshape(1, ROWS),
        segments.reshape(1, ROWS),
    )


def grad_kernel(*refs):
    q_refs = refs[:PIECES]
    (kv_ref, dkv_ref, own_ref, other_ref) = refs[PIECES : PIECES + 4]
    (qs, rows, dk, dv, dq, ints, ints_s, sem) = refs[PIECES + 4 :]
    scale = HEAD ** (-0.5)
    half = QBLOCKS // 2

    tails = [kv_ref[d, ROWS : ROWS + STATS, 0:ROWS].astype(jnp.float32) for d in range(PLANE)]
    number = jnp.concatenate([tail[0:1] for tail in tails], axis=0)
    key_seg = jnp.concatenate([tail[1:2] for tail in tails], axis=0)
    column = jnp.concatenate([number[:, 0:1], number[:, BLOCK : BLOCK + 1]], axis=0)
    column = jnp.broadcast_to(column, (KBLOCKS, ROWS))
    pad = jnp.full((ROWS - KBLOCKS, ROWS), FAR, jnp.float32)
    line = jnp.concatenate([column, pad], axis=0).T
    rank = jnp.sum((line[0:KBLOCKS] < column).astype(jnp.float32), axis=1, keepdims=True)
    lane = lax.broadcasted_iota(jnp.int32, (KBLOCKS, ROWS), 1).astype(jnp.float32)
    below_number = lax.broadcasted_iota(jnp.int32, (KBLOCKS, ROWS), 0).astype(jnp.float32)
    order = jnp.sum(
        jnp.where(rank == lane, below_number, 0.0), axis=0, keepdims=True
    )
    below = [
        jnp.sum((key_seg < float(s)).astype(jnp.float32), axis=0, keepdims=True) for s in range(1, 9)
    ]
    below = jnp.sum(jnp.concatenate(below, axis=0), axis=1, keepdims=True)
    below = jnp.broadcast_to(below, (8, STACK))
    segment = (lax.broadcasted_iota(jnp.int32, (8, STACK), 0) + 1).astype(jnp.float32)

    within = jnp.bitwise_and(lax.broadcasted_iota(jnp.int32, (1, STACK), 1), BLOCK - 1)
    within = within.astype(jnp.float32) + 1.0
    numbers, begins = [], []
    stats = []
    for qi in range(QBLOCKS):
        tail = q_refs[qi // 2][qi % 2, STACK : STACK + STATS, :].astype(jnp.float32)
        stat = tail[0:4] + tail[4:8] + tail[8:12]
        begin = jnp.max(jnp.where(stat[3:4] >= segment, below, 0.0), axis=0, keepdims=True)
        stats.append((stat, begin))
        numbers.append(stat[2:3, 0:1])
        begins.append(begin[:, 0:1])
    numbers = jnp.concatenate(numbers, axis=0)
    before = jnp.sum((line[0:QBLOCKS] < numbers).astype(jnp.float32), axis=1, keepdims=True)
    same = jnp.sum((line[0:QBLOCKS] == numbers).astype(jnp.float32), axis=1, keepdims=True)
    low = jnp.floor(jnp.concatenate(begins, axis=0) * (1.0 / BLOCK))
    steps = jnp.maximum(before + same - low, 0.0)
    steps = jnp.floor((steps + (TILE_BLOCKS - 1)) * (1.0 / TILE_BLOCKS))
    steps = jnp.broadcast_to(steps, (QBLOCKS, JOBS))
    row = lax.broadcasted_iota(jnp.int32, (QBLOCKS, JOBS), 0)
    done = steps
    for shift in (1, 2, 4, 8):
        done = done + jnp.where(row >= shift, pltpu.roll(done, shift, 0), 0.0)
    job = lax.broadcasted_iota(jnp.int32, (QBLOCKS, JOBS), 1).astype(jnp.float32)
    mine = (job < done) & (job >= done - steps)
    code = row.astype(jnp.float32) * 64.0 + low + (job - (done - steps)) * TILE_BLOCKS
    code = jnp.sum(jnp.where(mine, code, 0.0), axis=0, keepdims=True)
    count = done[QBLOCKS - 1 : QBLOCKS]
    code = jnp.where(job[0:1] < count, code, float(KBLOCKS))
    ints[0:1, :] = code.astype(jnp.int32)
    ints[1:2, 0:ROWS] = order.astype(jnp.int32)
    ints[2:3, :] = count.astype(jnp.int32)
    copy = pltpu.make_async_copy(ints, ints_s, sem)
    copy.start()

    for qi in range(QBLOCKS):
        stat, begin = stats[qi]
        rows[qi, 0:1, :] = stat[0:1]
        rows[qi, 1:2, :] = stat[1:2]
        rows[qi, 2:3, :] = begin
        qs[qi] = q_refs[qi // 2][qi % 2, 0:STACK, :]
        rows[qi, 3:4, :] = before[qi : qi + 1] * float(BLOCK) + same[qi : qi + 1] * within
    dk[...] = jnp.zeros_like(dk)
    dv[...] = jnp.zeros_like(dv)
    dq[...] = jnp.zeros_like(dq)
    copy.wait()

    count = ints_s[2, 0]
    down = lax.broadcasted_iota(jnp.int32, (TILE, ROWS), 0).astype(jnp.float32)
    nt = (((1,), (1,)), ((), ()))
    tn = (((0,), (0,)), ((), ()))

    def products(job):
        qi = jnp.right_shift(job, 6)
        at = jnp.bitwise_and(job, 63)
        blocks = [ints_s[1, at + i] for i in range(TILE_BLOCKS)]
        kv = jnp.concatenate(
            [
                kv_ref[
                    jnp.bitwise_and(j, PLANE - 1),
                    pl.ds(pl.multiple_of(jnp.right_shift(j, 4) * BLOCK, BLOCK), BLOCK),
                    :,
                ]
                for j in blocks
            ],
            axis=0,
        )
        k, v = kv[:, 0:HEAD], kv[:, HEAD : 2 * HEAD]
        q, g = qs[qi, :, 0:HEAD], qs[qi, :, HEAD : 2 * HEAD]
        s = lax.dot_general(k, q, nt, preferred_element_type=jnp.float32)
        gp = lax.dot_general(v, g, nt, preferred_element_type=jnp.float32)
        offset = (at * BLOCK).astype(jnp.float32)
        begin = rows[qi, 2:3, 0:ROWS] - offset
        end = rows[qi, 3:4, 0:ROWS] - offset
        seen = (down >= begin) & (down < end)
        seen = jnp.concatenate([seen, seen], axis=1)
        w = jnp.where(seen, jnp.exp2(s * (scale * LOG2E) - rows[qi, 0:1, :]), 0.0)
        ds = (w * (gp - rows[qi, 1:2, :]) * scale).astype(jnp.bfloat16)
        dv_part = jnp.dot(w.astype(jnp.bfloat16), g, preferred_element_type=jnp.float32)
        dk_part = jnp.dot(ds, q, preferred_element_type=jnp.float32)
        dq_part = lax.dot_general(k, ds, tn, preferred_element_type=jnp.float32)
        return qi, blocks, dq_part, dk_part, dv_part

    def jobs_step(step, carry):
        done = [products(ints_s[0, step * TOGETHER + i]) for i in range(TOGETHER)]
        for qi, blocks, dq_part, dk_part, dv_part in done:
            dq[qi] += dq_part
            for i, j in enumerate(blocks):
                part = slice(i * BLOCK, (i + 1) * BLOCK)
                dk[j] += dk_part[part]
                dv[j] += dv_part[part]
        return carry

    lax.fori_loop(0, lax.div(count + TOGETHER - 1, TOGETHER), jobs_step, 0)

    for j in range(KBLOCKS):
        d, to = j % PLANE, slice((j // PLANE) * BLOCK, (j // PLANE + 1) * BLOCK)
        dkv_ref[d, to, 0:HEAD] = dk[j].astype(jnp.bfloat16)
        dkv_ref[d, to, HEAD : 2 * HEAD] = dv[j].astype(jnp.bfloat16)
    for qi in range(half):
        own_ref[qi] = dq[qi].astype(jnp.bfloat16).T
        other_ref[qi] = dq[half + qi].astype(jnp.bfloat16).T


def grads(pieces, kv):
    half = QBLOCKS // 2
    return pl.pallas_call(
        grad_kernel,
        out_shape=(
            jax.ShapeDtypeStruct((PLANE, ROWS, 2 * HEAD), jnp.bfloat16),
            jax.ShapeDtypeStruct((half, STACK, HEAD), jnp.bfloat16),
            jax.ShapeDtypeStruct((half, STACK, HEAD), jnp.bfloat16),
        ),
        in_specs=[pl.BlockSpec(memory_space=pltpu.VMEM)] * (PIECES + 1),
        out_specs=(pl.BlockSpec(memory_space=pltpu.VMEM),) * 3,
        scratch_shapes=[
            pltpu.VMEM((QBLOCKS, STACK, 2 * HEAD), jnp.bfloat16),
            pltpu.VMEM((QBLOCKS, 8, STACK), jnp.float32),
            pltpu.VMEM((KBLOCKS, BLOCK, HEAD), jnp.float32),
            pltpu.VMEM((KBLOCKS, BLOCK, HEAD), jnp.float32),
            pltpu.VMEM((QBLOCKS, HEAD, STACK), jnp.float32),
            pltpu.VMEM((8, JOBS), jnp.int32),
            pltpu.SMEM((8, JOBS), jnp.int32),
            pltpu.SemaphoreType.DMA,
        ],
        compiler_params=pltpu.CompilerParams(vmem_limit_bytes=49 * 1024 * 1024),
        name="grads",
    )(*pieces, kv)


def unstack(array):
    return array.reshape(2, QH, BLOCK, HEAD).transpose(0, 2, 1, 3).reshape(ROWS, QH * HEAD)


def body(queries, keys, values, saved_out, out_grad, log_sums, positions, segments):
    qmsg, kvmsg = pack(queries, out_grad, saved_out, keys, values, log_sums, positions, segments)
    column = [qmsg] + [along_z(qmsg, shift) for shift in (1, 2, 3)]
    kv = over_plane(kvmsg)
    column = column + [to_partner(piece) for piece in column]
    dkv, own, other = grads(column, kv)
    total = own.astype(jnp.float32) + to_partner(other).astype(jnp.float32)
    total = total.reshape(DEPTH, 2, STACK, HEAD)
    back = [along_z(total[shift].astype(jnp.bfloat16), -shift) for shift in (1, 2, 3)]
    parts = over_plane(dkv)
    grad_keys = jnp.sum(parts[:, :, :HEAD].astype(jnp.float32), axis=0)
    grad_values = jnp.sum(parts[:, :, HEAD:].astype(jnp.float32), axis=0)
    grad_queries = total[0]
    for part in back:
        grad_queries = grad_queries + part.astype(jnp.float32)
    return (unstack(grad_queries), grad_keys, grad_values)


def solution(mesh):
    rows2, rows1 = P(AXES, None), P(AXES)
    return jax.shard_map(
        body,
        mesh=mesh,
        in_specs=(rows2,) * 6 + (rows1,) * 2,
        out_specs=(rows2,) * 3,
        check_vma=False,
    )
```

```python
import math

import jax
import jax.numpy as jnp
from jax import lax
from jax.experimental import pallas as pl
from jax.experimental.pallas import tpu as pltpu
from jax.sharding import PartitionSpec as P

HEAD = 128
QH = 4
ROWS = 128
BLOCK = 64
STATS = 16
PLANE = 16
DEPTH = 4
PIECES = 2 * DEPTH
QBLOCKS = 2 * PIECES
KBLOCKS = 2 * PLANE
STACK = QH * BLOCK
TILE = 256
TILE_BLOCKS = TILE // BLOCK
SLOTS = 40
JOBS = 128
TOGETHER = 6
FAR = 1.0e9
AXES = ("outer", "inner")
LOG2E = math.log2(math.e)


def place(index):
    outer, inner = divmod(index, 32)
    return (inner // 16) * 2 + outer // 2, outer % 2, inner % 16


def index_of(z, core, spot):
    return ((z % 2) * 2 + core) * 32 + (z // 2) * 16 + spot


def along_z(array, shift):
    pairs = []
    for source in range(128):
        z, core, spot = place(source)
        pairs.append((source, index_of((z + shift) % DEPTH, core, spot)))
    return lax.ppermute(array, AXES, pairs)


def to_partner(array):
    pairs = []
    for source in range(128):
        z, core, spot = place(source)
        pairs.append((source, index_of(z, 1 - core, spot)))
    return lax.ppermute(array, AXES, pairs)


def over_plane(array):
    groups = [list(range(first, first + PLANE)) for first in (0, PLANE)]
    return lax.all_to_all(array, "inner", 0, 0, axis_index_groups=groups, tiled=True)


def pack_kernel(q_hbm, g_hbm, o_hbm, k_hbm, v_hbm, lse_hbm, pos_hbm, seg_hbm, qmsg_ref, kvmsg_ref, *scratch):
    (q_ref, g_ref, o_ref, k_ref, v_ref, lse_ref, pos_ref, seg_ref, sems) = scratch
    sources = (lse_hbm, pos_hbm, seg_hbm, g_hbm, o_hbm, q_hbm, k_hbm, v_hbm)
    targets = (lse_ref, pos_ref, seg_ref, g_ref, o_ref, q_ref, k_ref, v_ref)
    copies = [pltpu.make_async_copy(s, t, sems.at[i]) for i, (s, t) in enumerate(zip(sources, targets))]
    for copy in copies:
        copy.start()
    for copy in copies:
        copy.wait()
    row = lax.broadcasted_iota(jnp.int32, (8, ROWS), 0)
    lane = lax.broadcasted_iota(jnp.int32, (8, ROWS), 1)
    block = jnp.right_shift(pos_ref[...], 6).astype(jnp.float32)
    seg = seg_ref[...].astype(jnp.float32)
    tops = []
    for h in range(QH):
        cols = slice(h * HEAD, (h + 1) * HEAD)
        prod = g_ref[:, cols].astype(jnp.float32) * o_ref[:, cols].astype(jnp.float32)
        dot = jnp.sum(prod.T, axis=0, keepdims=True)
        lse = lse_ref[h : h + 1, :] * LOG2E
        tops.append(
            jnp.where(
                row == 0,
                lse,
                jnp.where(row == 1, dot, jnp.where(row == 2, block, jnp.where(row == 3, seg, 0.0))),
            )
        )
        for b in range(2):
            to = slice(h * BLOCK, (h + 1) * BLOCK)
            frm = slice(b * BLOCK, (b + 1) * BLOCK)
            qmsg_ref[b, to, 0:HEAD] = q_ref[frm, cols]
            qmsg_ref[b, to, HEAD : 2 * HEAD] = g_ref[frm, cols]
    for pair in range(2):
        first, second = tops[2 * pair], tops[2 * pair + 1]
        halves = (
            jnp.where(lane < BLOCK, first, pltpu.roll(second, BLOCK, 1)),
            jnp.where(lane < BLOCK, pltpu.roll(first, BLOCK, 1), second),
        )
        for b in range(2):
            full = halves[b]
            high = full.astype(jnp.bfloat16).astype(jnp.float32)
            middle = (full - high).astype(jnp.bfloat16).astype(jnp.float32)
            low = full - high - middle
            upper = jnp.where(row < 4, high, pltpu.roll(middle, 4, 0))
            lower = jnp.where(row < 4, low, 0.0)
            qmsg_ref[b, STACK : STACK + STATS, pair * ROWS : (pair + 1) * ROWS] = jnp.concatenate(
                [upper, lower], axis=0
            ).astype(jnp.bfloat16)
    tail = jnp.where(row == 0, block, jnp.where(row == 1, seg, 0.0))
    tail = jnp.concatenate([tail, jnp.zeros_like(tail)], axis=0).astype(jnp.bfloat16)
    for d in range(PLANE):
        kvmsg_ref[d, 0:ROWS, 0:HEAD] = k_ref[...]
        kvmsg_ref[d, 0:ROWS, HEAD : 2 * HEAD] = v_ref[...]
        kvmsg_ref[d, ROWS : ROWS + STATS, 0:ROWS] = tail
        kvmsg_ref[d, ROWS : ROWS + STATS, ROWS : 2 * ROWS] = jnp.zeros_like(tail)


def pack(queries, out_grad, saved_out, keys, values, log_sums, positions, segments):
    wide = pltpu.VMEM((ROWS, QH * HEAD), jnp.bfloat16)
    narrow = pltpu.VMEM((ROWS, HEAD), jnp.bfloat16)
    line = pltpu.VMEM((1, ROWS), jnp.int32)
    return pl.pallas_call(
        pack_kernel,
        out_shape=(
            jax.ShapeDtypeStruct((2, STACK + STATS, 2 * HEAD), jnp.bfloat16),
            jax.ShapeDtypeStruct((PLANE, ROWS + STATS, 2 * HEAD), jnp.bfloat16),
        ),
        in_specs=[pl.BlockSpec(memory_space=pltpu.HBM)] * 8,
        out_specs=(pl.BlockSpec(memory_space=pltpu.VMEM),) * 2,
        scratch_shapes=[
            wide,
            wide,
            wide,
            narrow,
            narrow,
            pltpu.VMEM((QH, ROWS), jnp.float32),
            line,
            line,
            pltpu.SemaphoreType.DMA((8,)),
        ],
        compiler_params=pltpu.CompilerParams(vmem_limit_bytes=56 * 1024 * 1024),
        name="pack",
    )(
        queries,
        out_grad,
        saved_out,
        keys,
        values,
        log_sums.T,
        positions.reshape(1, ROWS),
        segments.reshape(1, ROWS),
    )


def grad_kernel(*refs):
    q_refs = refs[:PIECES]
    (kv_ref, dkv_ref, own_ref, other_ref) = refs[PIECES : PIECES + 4]
    (qs, rows, dk, dv, dq, jobs) = refs[PIECES + 4 :]
    scale = HEAD ** (-0.5)
    half = QBLOCKS // 2

    tails = [kv_ref[d, ROWS : ROWS + STATS, 0:ROWS].astype(jnp.float32) for d in range(PLANE)]
    number = jnp.concatenate([tail[0:1] for tail in tails], axis=0)
    key_seg = jnp.concatenate([tail[1:2] for tail in tails], axis=0)
    column = jnp.concatenate([number[:, 0:1], number[:, BLOCK : BLOCK + 1]], axis=0)
    column = jnp.broadcast_to(column, (KBLOCKS, ROWS))
    pad = jnp.full((ROWS - KBLOCKS, ROWS), FAR, jnp.float32)
    line = jnp.concatenate([column, pad], axis=0).T
    rank = jnp.sum((line[0:KBLOCKS] < column).astype(jnp.float32), axis=1, keepdims=True)
    lane = lax.broadcasted_iota(jnp.int32, (KBLOCKS, ROWS), 1).astype(jnp.float32)
    below_number = lax.broadcasted_iota(jnp.int32, (KBLOCKS, ROWS), 0).astype(jnp.float32)
    order = jnp.sum(
        jnp.where(rank == lane, below_number, 0.0), axis=0, keepdims=True
    )
    order = jnp.broadcast_to(order, (ROWS, ROWS)).T[0:SLOTS]
    below = [
        jnp.sum((key_seg < float(s)).astype(jnp.float32), axis=0, keepdims=True) for s in range(1, 9)
    ]
    below = jnp.sum(jnp.concatenate(below, axis=0), axis=1, keepdims=True)
    below = jnp.broadcast_to(below, (8, STACK))
    segment = (lax.broadcasted_iota(jnp.int32, (8, STACK), 0) + 1).astype(jnp.float32)

    within = jnp.bitwise_and(lax.broadcasted_iota(jnp.int32, (1, STACK), 1), BLOCK - 1)
    within = within.astype(jnp.float32) + 1.0
    numbers, begins = [], []
    stats = []
    for qi in range(QBLOCKS):
        tail = q_refs[qi // 2][qi % 2, STACK : STACK + STATS, :].astype(jnp.float32)
        stat = tail[0:4] + tail[4:8] + tail[8:12]
        begin = jnp.max(jnp.where(stat[3:4] >= segment, below, 0.0), axis=0, keepdims=True)
        stats.append((stat, begin))
        numbers.append(stat[2:3, 0:1])
        begins.append(begin[:, 0:1])
    numbers = jnp.concatenate(numbers, axis=0)
    before = jnp.sum((line[0:QBLOCKS] < numbers).astype(jnp.float32), axis=1, keepdims=True)
    same = jnp.sum((line[0:QBLOCKS] == numbers).astype(jnp.float32), axis=1, keepdims=True)
    low = jnp.floor(jnp.concatenate(begins, axis=0) * (1.0 / BLOCK))
    steps = jnp.maximum(before + same - low, 0.0)
    steps = jnp.floor((steps + (TILE_BLOCKS - 1)) * (1.0 / TILE_BLOCKS))
    steps = jnp.broadcast_to(steps, (QBLOCKS, JOBS))
    row = lax.broadcasted_iota(jnp.int32, (QBLOCKS, JOBS), 0)
    done = steps
    for shift in (1, 2, 4, 8):
        done = done + jnp.where(row >= shift, pltpu.roll(done, shift, 0), 0.0)
    job = lax.broadcasted_iota(jnp.int32, (QBLOCKS, JOBS), 1).astype(jnp.float32)
    mine = (job < done) & (job >= done - steps)
    code = row.astype(jnp.float32) * 64.0 + low + (job - (done - steps)) * TILE_BLOCKS
    code = jnp.sum(jnp.where(mine, code, 0.0), axis=0, keepdims=True)
    count = done[QBLOCKS - 1 : QBLOCKS]
    code = jnp.where(job[0:1] < count, code, float(KBLOCKS))
    query = jnp.floor(code * (1.0 / 64.0))
    at = code - query * 64.0
    slot = lax.broadcasted_iota(jnp.int32, (SLOTS, JOBS), 0).astype(jnp.float32)
    members = [
        jnp.sum(jnp.where(slot == at + float(i), order, 0.0), axis=0, keepdims=True)
        for i in range(TILE_BLOCKS)
    ]
    members = jnp.concatenate([query, at] + members + [jnp.zeros((2, JOBS), jnp.float32)], axis=0)
    pad = jnp.zeros((JOBS - 8, JOBS), jnp.float32)
    jobs[0:JOBS, :] = jnp.concatenate([members, pad], axis=0).T.astype(jnp.int32)
    jobs[JOBS : JOBS + 16, :] = jnp.where(
        lax.broadcasted_iota(jnp.int32, (16, ROWS), 1) == 1, KBLOCKS, 0
    )
    count = jnp.max(count).astype(jnp.int32)

    for qi in range(QBLOCKS):
        stat, begin = stats[qi]
        rows[qi, 0:1, :] = stat[0:1]
        rows[qi, 1:2, :] = stat[1:2]
        rows[qi, 2:3, :] = begin
        qs[qi] = q_refs[qi // 2][qi % 2, 0:STACK, :]
        rows[qi, 3:4, :] = before[qi : qi + 1] * float(BLOCK) + same[qi : qi + 1] * within
    dk[...] = jnp.zeros_like(dk)
    dv[...] = jnp.zeros_like(dv)
    dq[...] = jnp.zeros_like(dq)

    down = lax.broadcasted_iota(jnp.int32, (TILE, ROWS), 0).astype(jnp.float32)
    nt = (((1,), (1,)), ((), ()))
    tn = (((0,), (0,)), ((), ()))

    def products(record):
        qi, at, blocks = record[0], record[1], record[2:]
        kv = jnp.concatenate(
            [
                kv_ref[
                    jnp.bitwise_and(j, PLANE - 1),
                    pl.ds(pl.multiple_of(jnp.right_shift(j, 4) * BLOCK, BLOCK), BLOCK),
                    :,
                ]
                for j in blocks
            ],
            axis=0,
        )
        k, v = kv[:, 0:HEAD], kv[:, HEAD : 2 * HEAD]
        q, g = qs[qi, :, 0:HEAD], qs[qi, :, HEAD : 2 * HEAD]
        s = lax.dot_general(k, q, nt, preferred_element_type=jnp.float32)
        gp = lax.dot_general(v, g, nt, preferred_element_type=jnp.float32)
        offset = (at * BLOCK).astype(jnp.float32)
        begin = rows[qi, 2:3, 0:ROWS] - offset
        end = rows[qi, 3:4, 0:ROWS] - offset
        seen = (down >= begin) & (down < end)
        seen = jnp.concatenate([seen, seen], axis=1)
        w = jnp.where(seen, jnp.exp2(s * (scale * LOG2E) - rows[qi, 0:1, :]), 0.0)
        ds = (w * (gp - rows[qi, 1:2, :]) * scale).astype(jnp.bfloat16)
        dv_part = jnp.dot(w.astype(jnp.bfloat16), g, preferred_element_type=jnp.float32)
        dk_part = jnp.dot(ds, q, preferred_element_type=jnp.float32)
        dq_part = lax.dot_general(k, ds, tn, preferred_element_type=jnp.float32)
        return qi, blocks, dq_part, dk_part, dv_part

    def records(step):
        found = jobs[pl.ds(step * TOGETHER, 8), :]
        return [[found[i, r] for r in range(2 + TILE_BLOCKS)] for i in range(TOGETHER)]

    def jobs_step(step, carry):
        later = records(step + 1)
        done = [products(record) for record in carry]
        for qi, blocks, dq_part, dk_part, dv_part in done:
            dq[qi] += dq_part
            for i, j in enumerate(blocks):
                part = slice(i * BLOCK, (i + 1) * BLOCK)
                dk[j] += dk_part[part]
                dv[j] += dv_part[part]
        return later

    lax.fori_loop(0, lax.div(count + TOGETHER - 1, TOGETHER), jobs_step, records(0))

    for j in range(KBLOCKS):
        d, to = j % PLANE, slice((j // PLANE) * BLOCK, (j // PLANE + 1) * BLOCK)
        dkv_ref[d, to, 0:HEAD] = dk[j].astype(jnp.bfloat16)
        dkv_ref[d, to, HEAD : 2 * HEAD] = dv[j].astype(jnp.bfloat16)
    for qi in range(half):
        own_ref[qi] = dq[qi].astype(jnp.bfloat16).T
        other_ref[qi] = dq[half + qi].astype(jnp.bfloat16).T


def grads(pieces, kv):
    half = QBLOCKS // 2
    return pl.pallas_call(
        grad_kernel,
        out_shape=(
            jax.ShapeDtypeStruct((PLANE, ROWS, 2 * HEAD), jnp.bfloat16),
            jax.ShapeDtypeStruct((half, STACK, HEAD), jnp.bfloat16),
            jax.ShapeDtypeStruct((half, STACK, HEAD), jnp.bfloat16),
        ),
        in_specs=[pl.BlockSpec(memory_space=pltpu.VMEM)] * (PIECES + 1),
        out_specs=(pl.BlockSpec(memory_space=pltpu.VMEM),) * 3,
        scratch_shapes=[
            pltpu.VMEM((QBLOCKS, STACK, 2 * HEAD), jnp.bfloat16),
            pltpu.VMEM((QBLOCKS, 8, STACK), jnp.float32),
            pltpu.VMEM((KBLOCKS, BLOCK, HEAD), jnp.float32),
            pltpu.VMEM((KBLOCKS, BLOCK, HEAD), jnp.float32),
            pltpu.VMEM((QBLOCKS, HEAD, STACK), jnp.float32),
            pltpu.VMEM((JOBS + 16, ROWS), jnp.int32),
        ],
        compiler_params=pltpu.CompilerParams(vmem_limit_bytes=49 * 1024 * 1024),
        name="grads",
    )(*pieces, kv)


def unstack(array):
    return array.reshape(2, QH, BLOCK, HEAD).transpose(0, 2, 1, 3).reshape(ROWS, QH * HEAD)


def body(queries, keys, values, saved_out, out_grad, log_sums, positions, segments):
    qmsg, kvmsg = pack(queries, out_grad, saved_out, keys, values, log_sums, positions, segments)
    column = [qmsg] + [along_z(qmsg, shift) for shift in (1, 2, 3)]
    kv = over_plane(kvmsg)
    column = column + [to_partner(piece) for piece in column]
    dkv, own, other = grads(column, kv)
    total = own.astype(jnp.float32) + to_partner(other).astype(jnp.float32)
    total = total.reshape(DEPTH, 2, STACK, HEAD)
    back = [along_z(total[shift].astype(jnp.bfloat16), -shift) for shift in (1, 2, 3)]
    parts = over_plane(dkv)
    grad_keys = jnp.sum(parts[:, :, :HEAD].astype(jnp.float32), axis=0)
    grad_values = jnp.sum(parts[:, :, HEAD:].astype(jnp.float32), axis=0)
    grad_queries = total[0]
    for part in back:
        grad_queries = grad_queries + part.astype(jnp.float32)
    return (unstack(grad_queries), grad_keys, grad_values)


def solution(mesh):
    rows2, rows1 = P(AXES, None), P(AXES)
    return jax.shard_map(
        body,
        mesh=mesh,
        in_specs=(rows2,) * 6 + (rows1,) * 2,
        out_specs=(rows2,) * 3,
        check_vma=False,
    )
```

```python
import math

import jax
import jax.numpy as jnp
from jax import lax
from jax.experimental import pallas as pl
from jax.experimental.pallas import tpu as pltpu
from jax.sharding import PartitionSpec as P

HEAD = 128
QH = 4
ROWS = 128
BLOCK = 64
STATS = 16
PLANE = 16
DEPTH = 4
PIECES = 2 * DEPTH
QBLOCKS = 2 * PIECES
KBLOCKS = 2 * PLANE
STACK = QH * BLOCK
TILE = 256
TILE_BLOCKS = TILE // BLOCK
SLOTS = 40
JOBS = 128
TOGETHER = 6
FAR = 1.0e9
AXES = ("outer", "inner")
LOG2E = math.log2(math.e)


def place(index):
    outer, inner = divmod(index, 32)
    return (inner // 16) * 2 + outer // 2, outer % 2, inner % 16


def index_of(z, core, spot):
    return ((z % 2) * 2 + core) * 32 + (z // 2) * 16 + spot


def along_z(array, shift):
    pairs = []
    for source in range(128):
        z, core, spot = place(source)
        pairs.append((source, index_of((z + shift) % DEPTH, core, spot)))
    return lax.ppermute(array, AXES, pairs)


def to_partner(array):
    pairs = []
    for source in range(128):
        z, core, spot = place(source)
        pairs.append((source, index_of(z, 1 - core, spot)))
    return lax.ppermute(array, AXES, pairs)


def over_plane(array):
    groups = [list(range(first, first + PLANE)) for first in (0, PLANE)]
    return lax.all_to_all(array, "inner", 0, 0, axis_index_groups=groups, tiled=True)


def pack_kernel(q_hbm, g_hbm, o_hbm, k_hbm, v_hbm, lse_hbm, pos_hbm, seg_hbm, qmsg_ref, kvmsg_ref, *scratch):
    (q_ref, g_ref, o_ref, k_ref, v_ref, lse_ref, pos_ref, seg_ref, sems) = scratch
    sources = (lse_hbm, pos_hbm, seg_hbm, g_hbm, o_hbm, q_hbm, k_hbm, v_hbm)
    targets = (lse_ref, pos_ref, seg_ref, g_ref, o_ref, q_ref, k_ref, v_ref)
    copies = [pltpu.make_async_copy(s, t, sems.at[i]) for i, (s, t) in enumerate(zip(sources, targets))]
    for copy in copies:
        copy.start()
    for copy in copies:
        copy.wait()
    row = lax.broadcasted_iota(jnp.int32, (8, ROWS), 0)
    lane = lax.broadcasted_iota(jnp.int32, (8, ROWS), 1)
    block = jnp.right_shift(pos_ref[...], 6).astype(jnp.float32)
    seg = seg_ref[...].astype(jnp.float32)
    tops = []
    for h in range(QH):
        cols = slice(h * HEAD, (h + 1) * HEAD)
        prod = g_ref[:, cols].astype(jnp.float32) * o_ref[:, cols].astype(jnp.float32)
        dot = jnp.sum(prod.T, axis=0, keepdims=True)
        lse = lse_ref[h : h + 1, :] * LOG2E
        tops.append(
            jnp.where(
                row == 0,
                lse,
                jnp.where(row == 1, dot, jnp.where(row == 2, block, jnp.where(row == 3, seg, 0.0))),
            )
        )
        for b in range(2):
            to = slice(h * BLOCK, (h + 1) * BLOCK)
            frm = slice(b * BLOCK, (b + 1) * BLOCK)
            qmsg_ref[b, to, 0:HEAD] = q_ref[frm, cols]
            qmsg_ref[b, to, HEAD : 2 * HEAD] = g_ref[frm, cols]
    for pair in range(2):
        first, second = tops[2 * pair], tops[2 * pair + 1]
        halves = (
            jnp.where(lane < BLOCK, first, pltpu.roll(second, BLOCK, 1)),
            jnp.where(lane < BLOCK, pltpu.roll(first, BLOCK, 1), second),
        )
        for b in range(2):
            full = halves[b]
            high = full.astype(jnp.bfloat16).astype(jnp.float32)
            middle = (full - high).astype(jnp.bfloat16).astype(jnp.float32)
            low = full - high - middle
            upper = jnp.where(row < 4, high, pltpu.roll(middle, 4, 0))
            lower = jnp.where(row < 4, low, 0.0)
            qmsg_ref[b, STACK : STACK + STATS, pair * ROWS : (pair + 1) * ROWS] = jnp.concatenate(
                [upper, lower], axis=0
            ).astype(jnp.bfloat16)
    tail = jnp.where(row == 0, block, jnp.where(row == 1, seg, 0.0))
    tail = jnp.concatenate([tail, jnp.zeros_like(tail)], axis=0).astype(jnp.bfloat16)
    for d in range(PLANE):
        kvmsg_ref[d, 0:ROWS, 0:HEAD] = k_ref[...]
        kvmsg_ref[d, 0:ROWS, HEAD : 2 * HEAD] = v_ref[...]
        kvmsg_ref[d, ROWS : ROWS + STATS, 0:ROWS] = tail
        kvmsg_ref[d, ROWS : ROWS + STATS, ROWS : 2 * ROWS] = jnp.zeros_like(tail)


def pack(queries, out_grad, saved_out, keys, values, log_sums, positions, segments):
    wide = pltpu.VMEM((ROWS, QH * HEAD), jnp.bfloat16)
    narrow = pltpu.VMEM((ROWS, HEAD), jnp.bfloat16)
    line = pltpu.VMEM((1, ROWS), jnp.int32)
    return pl.pallas_call(
        pack_kernel,
        out_shape=(
            jax.ShapeDtypeStruct((2, STACK + STATS, 2 * HEAD), jnp.bfloat16),
            jax.ShapeDtypeStruct((PLANE, ROWS + STATS, 2 * HEAD), jnp.bfloat16),
        ),
        in_specs=[pl.BlockSpec(memory_space=pltpu.HBM)] * 8,
        out_specs=(pl.BlockSpec(memory_space=pltpu.VMEM),) * 2,
        scratch_shapes=[
            wide,
            wide,
            wide,
            narrow,
            narrow,
            pltpu.VMEM((QH, ROWS), jnp.float32),
            line,
            line,
            pltpu.SemaphoreType.DMA((8,)),
        ],
        compiler_params=pltpu.CompilerParams(vmem_limit_bytes=56 * 1024 * 1024),
        name="pack",
    )(
        queries,
        out_grad,
        saved_out,
        keys,
        values,
        log_sums.T,
        positions.reshape(1, ROWS),
        segments.reshape(1, ROWS),
    )


def grad_kernel(*refs):
    q_refs = refs[:PIECES]
    (kv_ref, dkv_ref, own_ref, other_ref) = refs[PIECES : PIECES + 4]
    (qs, rows, dk, dv, dq, jobs, stage, sems) = refs[PIECES + 4 :]
    scale = HEAD ** (-0.5)
    half = QBLOCKS // 2

    tails = [kv_ref[d, ROWS : ROWS + STATS, 0:ROWS].astype(jnp.float32) for d in range(PLANE)]
    number = jnp.concatenate([tail[0:1] for tail in tails], axis=0)
    key_seg = jnp.concatenate([tail[1:2] for tail in tails], axis=0)
    column = jnp.concatenate([number[:, 0:1], number[:, BLOCK : BLOCK + 1]], axis=0)
    column = jnp.broadcast_to(column, (KBLOCKS, ROWS))
    pad = jnp.full((ROWS - KBLOCKS, ROWS), FAR, jnp.float32)
    line = jnp.concatenate([column, pad], axis=0).T
    rank = jnp.sum((line[0:KBLOCKS] < column).astype(jnp.float32), axis=1, keepdims=True)
    lane = lax.broadcasted_iota(jnp.int32, (KBLOCKS, ROWS), 1).astype(jnp.float32)
    below_number = lax.broadcasted_iota(jnp.int32, (KBLOCKS, ROWS), 0).astype(jnp.float32)
    order = jnp.sum(
        jnp.where(rank == lane, below_number, 0.0), axis=0, keepdims=True
    )
    order = jnp.broadcast_to(order, (ROWS, ROWS)).T[0:SLOTS]
    below = [
        jnp.sum((key_seg < float(s)).astype(jnp.float32), axis=0, keepdims=True) for s in range(1, 9)
    ]
    below = jnp.sum(jnp.concatenate(below, axis=0), axis=1, keepdims=True)
    below = jnp.broadcast_to(below, (8, STACK))
    segment = (lax.broadcasted_iota(jnp.int32, (8, STACK), 0) + 1).astype(jnp.float32)

    within = jnp.bitwise_and(lax.broadcasted_iota(jnp.int32, (1, STACK), 1), BLOCK - 1)
    within = within.astype(jnp.float32) + 1.0
    numbers, begins = [], []
    stats = []
    for qi in range(QBLOCKS):
        tail = q_refs[qi // 2][qi % 2, STACK : STACK + STATS, :].astype(jnp.float32)
        stat = tail[0:4] + tail[4:8] + tail[8:12]
        begin = jnp.max(jnp.where(stat[3:4] >= segment, below, 0.0), axis=0, keepdims=True)
        stats.append((stat, begin))
        numbers.append(stat[2:3, 0:1])
        begins.append(begin[:, 0:1])
    numbers = jnp.concatenate(numbers, axis=0)
    before = jnp.sum((line[0:QBLOCKS] < numbers).astype(jnp.float32), axis=1, keepdims=True)
    same = jnp.sum((line[0:QBLOCKS] == numbers).astype(jnp.float32), axis=1, keepdims=True)
    low = jnp.floor(jnp.concatenate(begins, axis=0) * (1.0 / BLOCK))
    steps = jnp.maximum(before + same - low, 0.0)
    steps = jnp.floor((steps + (TILE_BLOCKS - 1)) * (1.0 / TILE_BLOCKS))
    steps = jnp.broadcast_to(steps, (QBLOCKS, JOBS))
    row = lax.broadcasted_iota(jnp.int32, (QBLOCKS, JOBS), 0)
    done = steps
    for shift in (1, 2, 4, 8):
        done = done + jnp.where(row >= shift, pltpu.roll(done, shift, 0), 0.0)
    job = lax.broadcasted_iota(jnp.int32, (QBLOCKS, JOBS), 1).astype(jnp.float32)
    mine = (job < done) & (job >= done - steps)
    code = row.astype(jnp.float32) * 64.0 + low + (job - (done - steps)) * TILE_BLOCKS
    code = jnp.sum(jnp.where(mine, code, 0.0), axis=0, keepdims=True)
    count = done[QBLOCKS - 1 : QBLOCKS]
    code = jnp.where(job[0:1] < count, code, float(KBLOCKS))
    query = jnp.floor(code * (1.0 / 64.0))
    at = code - query * 64.0
    slot = lax.broadcasted_iota(jnp.int32, (SLOTS, JOBS), 0).astype(jnp.float32)
    members = [
        jnp.sum(jnp.where(slot == at + float(i), order, 0.0), axis=0, keepdims=True)
        for i in range(TILE_BLOCKS)
    ]
    members = jnp.concatenate([query, at] + members + [jnp.zeros((2, JOBS), jnp.float32)], axis=0)
    pad = jnp.zeros((JOBS - 8, JOBS), jnp.float32)
    jobs[0:JOBS, :] = jnp.concatenate([members, pad], axis=0).T.astype(jnp.int32)
    jobs[JOBS : JOBS + 16, :] = jnp.where(
        lax.broadcasted_iota(jnp.int32, (16, ROWS), 1) == 1, KBLOCKS, 0
    )
    count = jnp.max(count).astype(jnp.int32)

    for qi in range(QBLOCKS):
        stat, begin = stats[qi]
        rows[qi, 0:1, :] = stat[0:1]
        rows[qi, 1:2, :] = stat[1:2]
        rows[qi, 2:3, :] = begin
        qs[qi] = q_refs[qi // 2][qi % 2, 0:STACK, :]
        rows[qi, 3:4, :] = before[qi : qi + 1] * float(BLOCK) + same[qi : qi + 1] * within
    dk[...] = jnp.zeros_like(dk)
    dv[...] = jnp.zeros_like(dv)
    dq[...] = jnp.zeros_like(dq)

    down = lax.broadcasted_iota(jnp.int32, (TILE, ROWS), 0).astype(jnp.float32)
    nt = (((1,), (1,)), ((), ()))
    tn = (((0,), (0,)), ((), ()))

    def products(record):
        qi, at, blocks = record[0], record[1], record[2:]
        kv = jnp.concatenate(
            [
                kv_ref[
                    jnp.bitwise_and(j, PLANE - 1),
                    pl.ds(pl.multiple_of(jnp.right_shift(j, 4) * BLOCK, BLOCK), BLOCK),
                    :,
                ]
                for j in blocks
            ],
            axis=0,
        )
        k, v = kv[:, 0:HEAD], kv[:, HEAD : 2 * HEAD]
        q, g = qs[qi, :, 0:HEAD], qs[qi, :, HEAD : 2 * HEAD]
        s = lax.dot_general(k, q, nt, preferred_element_type=jnp.float32)
        gp = lax.dot_general(v, g, nt, preferred_element_type=jnp.float32)
        offset = (at * BLOCK).astype(jnp.float32)
        begin = rows[qi, 2:3, 0:ROWS] - offset
        end = rows[qi, 3:4, 0:ROWS] - offset
        seen = (down >= begin) & (down < end)
        seen = jnp.concatenate([seen, seen], axis=1)
        w = jnp.where(seen, jnp.exp2(s * (scale * LOG2E) - rows[qi, 0:1, :]), 0.0)
        ds = (w * (gp - rows[qi, 1:2, :]) * scale).astype(jnp.bfloat16)
        dv_part = jnp.dot(w.astype(jnp.bfloat16), g, preferred_element_type=jnp.float32)
        dk_part = jnp.dot(ds, q, preferred_element_type=jnp.float32)
        dq_part = lax.dot_general(k, ds, tn, preferred_element_type=jnp.float32)
        return qi, blocks, dq_part, dk_part, dv_part

    def records(step):
        found = jobs[pl.ds(step * TOGETHER, 8), :]
        return [[found[i, r] for r in range(2 + TILE_BLOCKS)] for i in range(TOGETHER)]

    def jobs_step(step, carry):
        later = records(step + 1)
        done = [products(record) for record in carry]
        for qi, blocks, dq_part, dk_part, dv_part in done:
            dq[qi] += dq_part
            for i, j in enumerate(blocks):
                part = slice(i * BLOCK, (i + 1) * BLOCK)
                dk[j] += dk_part[part]
                dv[j] += dv_part[part]
        return later

    lax.fori_loop(0, lax.div(count + TOGETHER - 1, TOGETHER), jobs_step, records(0))

    for d in range(PLANE):
        for b in range(2):
            to = slice(b * BLOCK, (b + 1) * BLOCK)
            stage[d, to, 0:HEAD] = dk[b * PLANE + d].astype(jnp.bfloat16)
            stage[d, to, HEAD : 2 * HEAD] = dv[b * PLANE + d].astype(jnp.bfloat16)
        pltpu.make_async_copy(stage.at[d], dkv_ref.at[d], sems.at[d]).start()
    for qi in range(half):
        own_ref[qi] = dq[qi].astype(jnp.bfloat16).T
        other_ref[qi] = dq[half + qi].astype(jnp.bfloat16).T
    for d in range(PLANE):
        pltpu.make_async_copy(stage.at[d], dkv_ref.at[d], sems.at[d]).wait()


def grads(pieces, kv):
    half = QBLOCKS // 2
    return pl.pallas_call(
        grad_kernel,
        out_shape=(
            jax.ShapeDtypeStruct((PLANE, ROWS, 2 * HEAD), jnp.bfloat16),
            jax.ShapeDtypeStruct((half, STACK, HEAD), jnp.bfloat16),
            jax.ShapeDtypeStruct((half, STACK, HEAD), jnp.bfloat16),
        ),
        in_specs=[pl.BlockSpec(memory_space=pltpu.VMEM)] * (PIECES + 1),
        out_specs=(pl.BlockSpec(memory_space=pl.ANY),)
        + (pl.BlockSpec(memory_space=pltpu.VMEM),) * 2,
        scratch_shapes=[
            pltpu.VMEM((QBLOCKS, STACK, 2 * HEAD), jnp.bfloat16),
            pltpu.VMEM((QBLOCKS, 8, STACK), jnp.float32),
            pltpu.VMEM((KBLOCKS, BLOCK, HEAD), jnp.float32),
            pltpu.VMEM((KBLOCKS, BLOCK, HEAD), jnp.float32),
            pltpu.VMEM((QBLOCKS, HEAD, STACK), jnp.float32),
            pltpu.VMEM((JOBS + 16, ROWS), jnp.int32),
            pltpu.VMEM((PLANE, ROWS, 2 * HEAD), jnp.bfloat16),
            pltpu.SemaphoreType.DMA((PLANE,)),
        ],
        compiler_params=pltpu.CompilerParams(vmem_limit_bytes=49 * 1024 * 1024),
        name="grads",
    )(*pieces, kv)


def unstack(array):
    return array.reshape(2, QH, BLOCK, HEAD).transpose(0, 2, 1, 3).reshape(ROWS, QH * HEAD)


def body(queries, keys, values, saved_out, out_grad, log_sums, positions, segments):
    qmsg, kvmsg = pack(queries, out_grad, saved_out, keys, values, log_sums, positions, segments)
    column = [qmsg] + [along_z(qmsg, shift) for shift in (1, 2, 3)]
    kv = over_plane(kvmsg)
    column = column + [to_partner(piece) for piece in column]
    dkv, own, other = grads(column, kv)
    total = own.astype(jnp.float32) + to_partner(other).astype(jnp.float32)
    total = total.reshape(DEPTH, 2, STACK, HEAD)
    back = [along_z(total[shift].astype(jnp.bfloat16), -shift) for shift in (1, 2, 3)]
    parts = over_plane(dkv)
    grad_keys = jnp.sum(parts[:, :, :HEAD].astype(jnp.float32), axis=0)
    grad_values = jnp.sum(parts[:, :, HEAD:].astype(jnp.float32), axis=0)
    grad_queries = total[0]
    for part in back:
        grad_queries = grad_queries + part.astype(jnp.float32)
    return (unstack(grad_queries), grad_keys, grad_values)


def solution(mesh):
    rows2, rows1 = P(AXES, None), P(AXES)
    return jax.shard_map(
        body,
        mesh=mesh,
        in_specs=(rows2,) * 6 + (rows1,) * 2,
        out_specs=(rows2,) * 3,
        check_vma=False,
    )
```

```python
import math

import jax
import jax.numpy as jnp
from jax import lax
from jax.experimental import pallas as pl
from jax.experimental.pallas import tpu as pltpu
from jax.sharding import PartitionSpec as P

HEAD = 128
QH = 4
ROWS = 128
BLOCK = 64
STATS = 16
PLANE = 16
DEPTH = 4
PIECES = 2 * DEPTH
QBLOCKS = 2 * PIECES
KBLOCKS = 2 * PLANE
STACK = QH * BLOCK
TILE = 256
TILE_BLOCKS = TILE // BLOCK
SLOTS = 40
JOBS = 128
TOGETHER = 6
FAR = 1.0e9
AXES = ("outer", "inner")
LOG2E = math.log2(math.e)


def place(index):
    outer, inner = divmod(index, 32)
    return (inner // 16) * 2 + outer // 2, outer % 2, inner % 16


def index_of(z, core, spot):
    return ((z % 2) * 2 + core) * 32 + (z // 2) * 16 + spot


def along_z(array, shift):
    pairs = []
    for source in range(128):
        z, core, spot = place(source)
        pairs.append((source, index_of((z + shift) % DEPTH, core, spot)))
    return lax.ppermute(array, AXES, pairs)


def to_partner(array):
    pairs = []
    for source in range(128):
        z, core, spot = place(source)
        pairs.append((source, index_of(z, 1 - core, spot)))
    return lax.ppermute(array, AXES, pairs)


def over_plane(array):
    groups = [list(range(first, first + PLANE)) for first in (0, PLANE)]
    return lax.all_to_all(array, "inner", 0, 0, axis_index_groups=groups, tiled=True)


def pack_kernel(q_hbm, g_hbm, o_hbm, k_hbm, v_hbm, lse_hbm, pos_hbm, seg_hbm, qmsg_ref, kvmsg_ref, *scratch):
    (q_ref, g_ref, o_ref, k_ref, v_ref, lse_ref, pos_ref, seg_ref, sems) = scratch
    sources = (lse_hbm, pos_hbm, seg_hbm, g_hbm, o_hbm, q_hbm, k_hbm, v_hbm)
    targets = (lse_ref, pos_ref, seg_ref, g_ref, o_ref, q_ref, k_ref, v_ref)
    copies = [pltpu.make_async_copy(s, t, sems.at[i]) for i, (s, t) in enumerate(zip(sources, targets))]
    for copy in copies:
        copy.start()
    for copy in copies[:5]:
        copy.wait()
    row = lax.broadcasted_iota(jnp.int32, (8, ROWS), 0)
    lane = lax.broadcasted_iota(jnp.int32, (8, ROWS), 1)
    block = jnp.right_shift(pos_ref[...], 6).astype(jnp.float32)
    seg = seg_ref[...].astype(jnp.float32)
    tops = []
    for h in range(QH):
        cols = slice(h * HEAD, (h + 1) * HEAD)
        prod = g_ref[:, cols].astype(jnp.float32) * o_ref[:, cols].astype(jnp.float32)
        dot = jnp.sum(prod.T, axis=0, keepdims=True)
        lse = lse_ref[h : h + 1, :] * LOG2E
        tops.append(
            jnp.where(
                row == 0,
                lse,
                jnp.where(row == 1, dot, jnp.where(row == 2, block, jnp.where(row == 3, seg, 0.0))),
            )
        )
    for copy in copies[5:]:
        copy.wait()
    for h in range(QH):
        cols = slice(h * HEAD, (h + 1) * HEAD)
        for b in range(2):
            to = slice(h * BLOCK, (h + 1) * BLOCK)
            frm = slice(b * BLOCK, (b + 1) * BLOCK)
            qmsg_ref[b, to, 0:HEAD] = q_ref[frm, cols]
            qmsg_ref[b, to, HEAD : 2 * HEAD] = g_ref[frm, cols]
    for pair in range(2):
        first, second = tops[2 * pair], tops[2 * pair + 1]
        halves = (
            jnp.where(lane < BLOCK, first, pltpu.roll(second, BLOCK, 1)),
            jnp.where(lane < BLOCK, pltpu.roll(first, BLOCK, 1), second),
        )
        for b in range(2):
            full = halves[b]
            high = full.astype(jnp.bfloat16).astype(jnp.float32)
            middle = (full - high).astype(jnp.bfloat16).astype(jnp.float32)
            low = full - high - middle
            upper = jnp.where(row < 4, high, pltpu.roll(middle, 4, 0))
            lower = jnp.where(row < 4, low, 0.0)
            qmsg_ref[b, STACK : STACK + STATS, pair * ROWS : (pair + 1) * ROWS] = jnp.concatenate(
                [upper, lower], axis=0
            ).astype(jnp.bfloat16)
    tail = jnp.where(row == 0, block, jnp.where(row == 1, seg, 0.0))
    tail = jnp.concatenate([tail, jnp.zeros_like(tail)], axis=0).astype(jnp.bfloat16)
    for d in range(PLANE):
        kvmsg_ref[d, 0:ROWS, 0:HEAD] = k_ref[...]
        kvmsg_ref[d, 0:ROWS, HEAD : 2 * HEAD] = v_ref[...]
        kvmsg_ref[d, ROWS : ROWS + STATS, 0:ROWS] = tail
        kvmsg_ref[d, ROWS : ROWS + STATS, ROWS : 2 * ROWS] = jnp.zeros_like(tail)


def pack(queries, out_grad, saved_out, keys, values, log_sums, positions, segments):
    wide = pltpu.VMEM((ROWS, QH * HEAD), jnp.bfloat16)
    narrow = pltpu.VMEM((ROWS, HEAD), jnp.bfloat16)
    line = pltpu.VMEM((1, ROWS), jnp.int32)
    return pl.pallas_call(
        pack_kernel,
        out_shape=(
            jax.ShapeDtypeStruct((2, STACK + STATS, 2 * HEAD), jnp.bfloat16),
            jax.ShapeDtypeStruct((PLANE, ROWS + STATS, 2 * HEAD), jnp.bfloat16),
        ),
        in_specs=[pl.BlockSpec(memory_space=pltpu.HBM)] * 8,
        out_specs=(pl.BlockSpec(memory_space=pltpu.VMEM),) * 2,
        scratch_shapes=[
            wide,
            wide,
            wide,
            narrow,
            narrow,
            pltpu.VMEM((QH, ROWS), jnp.float32),
            line,
            line,
            pltpu.SemaphoreType.DMA((8,)),
        ],
        compiler_params=pltpu.CompilerParams(vmem_limit_bytes=56 * 1024 * 1024),
        name="pack",
    )(
        queries,
        out_grad,
        saved_out,
        keys,
        values,
        log_sums.T,
        positions.reshape(1, ROWS),
        segments.reshape(1, ROWS),
    )


def grad_kernel(*refs):
    q_refs = refs[:PIECES]
    (kv_ref, dkv_ref, own_ref, other_ref) = refs[PIECES : PIECES + 4]
    (qs, rows, dk, dv, dq, jobs, stage, sems) = refs[PIECES + 4 :]
    scale = HEAD ** (-0.5)
    half = QBLOCKS // 2

    tails = [kv_ref[d, ROWS : ROWS + STATS, 0:ROWS].astype(jnp.float32) for d in range(PLANE)]
    number = jnp.concatenate([tail[0:1] for tail in tails], axis=0)
    key_seg = jnp.concatenate([tail[1:2] for tail in tails], axis=0)
    column = jnp.concatenate([number[:, 0:1], number[:, BLOCK : BLOCK + 1]], axis=0)
    column = jnp.broadcast_to(column, (KBLOCKS, ROWS))
    pad = jnp.full((ROWS - KBLOCKS, ROWS), FAR, jnp.float32)
    line = jnp.concatenate([column, pad], axis=0).T
    rank = jnp.sum((line[0:KBLOCKS] < column).astype(jnp.float32), axis=1, keepdims=True)
    lane = lax.broadcasted_iota(jnp.int32, (KBLOCKS, ROWS), 1).astype(jnp.float32)
    below_number = lax.broadcasted_iota(jnp.int32, (KBLOCKS, ROWS), 0).astype(jnp.float32)
    order = jnp.sum(
        jnp.where(rank == lane, below_number, 0.0), axis=0, keepdims=True
    )
    order = jnp.broadcast_to(order, (ROWS, ROWS)).T[0:SLOTS]
    below = [
        jnp.sum((key_seg < float(s)).astype(jnp.float32), axis=0, keepdims=True) for s in range(1, 9)
    ]
    below = jnp.sum(jnp.concatenate(below, axis=0), axis=1, keepdims=True)
    below = jnp.broadcast_to(below, (8, STACK))
    segment = (lax.broadcasted_iota(jnp.int32, (8, STACK), 0) + 1).astype(jnp.float32)

    within = jnp.bitwise_and(lax.broadcasted_iota(jnp.int32, (1, STACK), 1), BLOCK - 1)
    within = within.astype(jnp.float32) + 1.0
    numbers, begins = [], []
    stats = []
    for qi in range(QBLOCKS):
        tail = q_refs[qi // 2][qi % 2, STACK : STACK + STATS, :].astype(jnp.float32)
        stat = tail[0:4] + tail[4:8] + tail[8:12]
        begin = jnp.max(jnp.where(stat[3:4] >= segment, below, 0.0), axis=0, keepdims=True)
        stats.append((stat, begin))
        numbers.append(stat[2:3, 0:1])
        begins.append(begin[:, 0:1])
    numbers = jnp.concatenate(numbers, axis=0)
    before = jnp.sum((line[0:QBLOCKS] < numbers).astype(jnp.float32), axis=1, keepdims=True)
    same = jnp.sum((line[0:QBLOCKS] == numbers).astype(jnp.float32), axis=1, keepdims=True)
    low = jnp.floor(jnp.concatenate(begins, axis=0) * (1.0 / BLOCK))
    steps = jnp.maximum(before + same - low, 0.0)
    steps = jnp.floor((steps + (TILE_BLOCKS - 1)) * (1.0 / TILE_BLOCKS))
    steps = jnp.broadcast_to(steps, (QBLOCKS, JOBS))
    row = lax.broadcasted_iota(jnp.int32, (QBLOCKS, JOBS), 0)
    done = steps
    for shift in (1, 2, 4, 8):
        done = done + jnp.where(row >= shift, pltpu.roll(done, shift, 0), 0.0)
    job = lax.broadcasted_iota(jnp.int32, (QBLOCKS, JOBS), 1).astype(jnp.float32)
    mine = (job < done) & (job >= done - steps)
    code = row.astype(jnp.float32) * 64.0 + low + (job - (done - steps)) * TILE_BLOCKS
    code = jnp.sum(jnp.where(mine, code, 0.0), axis=0, keepdims=True)
    count = done[QBLOCKS - 1 : QBLOCKS]
    code = jnp.where(job[0:1] < count, code, float(KBLOCKS))
    query = jnp.floor(code * (1.0 / 64.0))
    at = code - query * 64.0
    slot = lax.broadcasted_iota(jnp.int32, (SLOTS, JOBS), 0).astype(jnp.float32)
    members = [
        jnp.sum(jnp.where(slot == at + float(i), order, 0.0), axis=0, keepdims=True)
        for i in range(TILE_BLOCKS)
    ]
    members = jnp.concatenate([query, at] + members + [jnp.zeros((2, JOBS), jnp.float32)], axis=0)
    pad = jnp.zeros((JOBS - 8, JOBS), jnp.float32)
    jobs[0:JOBS, :] = jnp.concatenate([members, pad], axis=0).T.astype(jnp.int32)
    jobs[JOBS : JOBS + 16, :] = jnp.where(
        lax.broadcasted_iota(jnp.int32, (16, ROWS), 1) == 1, KBLOCKS, 0
    )
    count = jnp.max(count).astype(jnp.int32)

    for qi in range(QBLOCKS):
        stat, begin = stats[qi]
        rows[qi, 0:1, :] = stat[0:1]
        rows[qi, 1:2, :] = stat[1:2]
        rows[qi, 2:3, :] = begin
        qs[qi] = q_refs[qi // 2][qi % 2, 0:STACK, :]
        rows[qi, 3:4, :] = before[qi : qi + 1] * float(BLOCK) + same[qi : qi + 1] * within
    dk[...] = jnp.zeros_like(dk)
    dv[...] = jnp.zeros_like(dv)
    dq[...] = jnp.zeros_like(dq)

    down = lax.broadcasted_iota(jnp.int32, (TILE, ROWS), 0).astype(jnp.float32)
    nt = (((1,), (1,)), ((), ()))
    tn = (((0,), (0,)), ((), ()))

    def products(record):
        qi, at, blocks = record[0], record[1], record[2:]
        kv = jnp.concatenate(
            [
                kv_ref[
                    jnp.bitwise_and(j, PLANE - 1),
                    pl.ds(pl.multiple_of(jnp.right_shift(j, 4) * BLOCK, BLOCK), BLOCK),
                    :,
                ]
                for j in blocks
            ],
            axis=0,
        )
        k, v = kv[:, 0:HEAD], kv[:, HEAD : 2 * HEAD]
        q, g = qs[qi, :, 0:HEAD], qs[qi, :, HEAD : 2 * HEAD]
        s = lax.dot_general(k, q, nt, preferred_element_type=jnp.float32)
        gp = lax.dot_general(v, g, nt, preferred_element_type=jnp.float32)
        offset = (at * BLOCK).astype(jnp.float32)
        begin = rows[qi, 2:3, 0:ROWS] - offset
        end = rows[qi, 3:4, 0:ROWS] - offset
        seen = (down >= begin) & (down < end)
        seen = jnp.concatenate([seen, seen], axis=1)
        w = jnp.where(seen, jnp.exp2(s * (scale * LOG2E) - rows[qi, 0:1, :]), 0.0)
        ds = (w * (gp - rows[qi, 1:2, :]) * scale).astype(jnp.bfloat16)
        dv_part = jnp.dot(w.astype(jnp.bfloat16), g, preferred_element_type=jnp.float32)
        dk_part = jnp.dot(ds, q, preferred_element_type=jnp.float32)
        dq_part = lax.dot_general(k, ds, tn, preferred_element_type=jnp.float32)
        return qi, blocks, dq_part, dk_part, dv_part

    def records(step):
        found = jobs[pl.ds(step * TOGETHER, 8), :]
        return [[found[i, r] for r in range(2 + TILE_BLOCKS)] for i in range(TOGETHER)]

    def jobs_step(step, carry):
        later = records(step + 1)
        done = [products(record) for record in carry]
        for qi, blocks, dq_part, dk_part, dv_part in done:
            dq[qi] += dq_part
            for i, j in enumerate(blocks):
                part = slice(i * BLOCK, (i + 1) * BLOCK)
                dk[j] += dk_part[part]
                dv[j] += dv_part[part]
        return later

    lax.fori_loop(0, lax.div(count + TOGETHER - 1, TOGETHER), jobs_step, records(0))

    for d in range(PLANE):
        for b in range(2):
            to = slice(b * BLOCK, (b + 1) * BLOCK)
            stage[d, to, 0:HEAD] = dk[b * PLANE + d].astype(jnp.bfloat16)
            stage[d, to, HEAD : 2 * HEAD] = dv[b * PLANE + d].astype(jnp.bfloat16)
        pltpu.make_async_copy(stage.at[d], dkv_ref.at[d], sems.at[d]).start()
    for qi in range(half):
        own_ref[qi] = dq[qi].astype(jnp.bfloat16).T
        other_ref[qi] = dq[half + qi].astype(jnp.bfloat16).T
    for d in range(PLANE):
        pltpu.make_async_copy(stage.at[d], dkv_ref.at[d], sems.at[d]).wait()


def grads(pieces, kv):
    half = QBLOCKS // 2
    return pl.pallas_call(
        grad_kernel,
        out_shape=(
            jax.ShapeDtypeStruct((PLANE, ROWS, 2 * HEAD), jnp.bfloat16),
            jax.ShapeDtypeStruct((half, STACK, HEAD), jnp.bfloat16),
            jax.ShapeDtypeStruct((half, STACK, HEAD), jnp.bfloat16),
        ),
        in_specs=[pl.BlockSpec(memory_space=pltpu.VMEM)] * (PIECES + 1),
        out_specs=(pl.BlockSpec(memory_space=pl.ANY),)
        + (pl.BlockSpec(memory_space=pltpu.VMEM),) * 2,
        scratch_shapes=[
            pltpu.VMEM((QBLOCKS, STACK, 2 * HEAD), jnp.bfloat16),
            pltpu.VMEM((QBLOCKS, 8, STACK), jnp.float32),
            pltpu.VMEM((KBLOCKS, BLOCK, HEAD), jnp.float32),
            pltpu.VMEM((KBLOCKS, BLOCK, HEAD), jnp.float32),
            pltpu.VMEM((QBLOCKS, HEAD, STACK), jnp.float32),
            pltpu.VMEM((JOBS + 16, ROWS), jnp.int32),
            pltpu.VMEM((PLANE, ROWS, 2 * HEAD), jnp.bfloat16),
            pltpu.SemaphoreType.DMA((PLANE,)),
        ],
        compiler_params=pltpu.CompilerParams(vmem_limit_bytes=49 * 1024 * 1024),
        name="grads",
    )(*pieces, kv)


def unstack(array):
    return array.reshape(2, QH, BLOCK, HEAD).transpose(0, 2, 1, 3).reshape(ROWS, QH * HEAD)


def body(queries, keys, values, saved_out, out_grad, log_sums, positions, segments):
    qmsg, kvmsg = pack(queries, out_grad, saved_out, keys, values, log_sums, positions, segments)
    column = [qmsg] + [along_z(qmsg, shift) for shift in (1, 2, 3)]
    kv = over_plane(kvmsg)
    column = column + [to_partner(piece) for piece in column]
    dkv, own, other = grads(column, kv)
    total = own.astype(jnp.float32) + to_partner(other).astype(jnp.float32)
    total = total.reshape(DEPTH, 2, STACK, HEAD)
    back = [along_z(total[shift].astype(jnp.bfloat16), -shift) for shift in (1, 2, 3)]
    parts = over_plane(dkv)
    grad_keys = jnp.sum(parts[:, :, :HEAD].astype(jnp.float32), axis=0)
    grad_values = jnp.sum(parts[:, :, HEAD:].astype(jnp.float32), axis=0)
    grad_queries = total[0]
    for part in back:
        grad_queries = grad_queries + part.astype(jnp.float32)
    return (unstack(grad_queries), grad_keys, grad_values)


def solution(mesh):
    rows2, rows1 = P(AXES, None), P(AXES)
    return jax.shard_map(
        body,
        mesh=mesh,
        in_specs=(rows2,) * 6 + (rows1,) * 2,
        out_specs=(rows2,) * 3,
        check_vma=False,
    )
```
